256 devices in a mesh: dp: 2 (over core), seq: 128 (over y, x, z).
Axes of the slice: x: 4, y: 4, z: 8, core: 2. Of those that a mesh axis runs over, the one named last changes fastest.
Arguments:
- activations: bfloat16 [4, 8192, 1024], P('dp', 'seq'), may hold values from -28 to 28
- segment_ids: int32 [4, 8192], P('dp', 'seq'), may hold values from 0 to 15, as said below
- interval_bounds: int32 [4, 17], P('dp'), may hold values from 0 to 8192, as said below
- conv_weight: bfloat16 [2, 1024, 1536], replicated, may hold values from -0.109375 to 0.109375
- proj_weight: bfloat16 [2, 1024, 512], replicated, may hold values from -0.25 to 0.25
- gains_in: float32 [2, 1024], replicated, may hold values from 0.25 to 1.75
- biases_in: float32 [2, 1024], replicated, may hold values from -2.5 to 2.5
- gains_mid: float32 [2, 512], replicated, may hold values from 0.25 to 1.75
- biases_mid: float32 [2, 512], replicated, may hold values from -2.5 to 2.5
- cotangent: bfloat16 [4, 8192, 1024], P('dp', 'seq'), may hold values from -24 to 24
Outputs:
- out_acts: bfloat16 [4, 8192, 1024], P('dp', 'seq')
- grad_acts: bfloat16 [4, 8192, 1024], P('dp', 'seq')
- grad_conv: float32 [2, 1024, 1536], P(None, 'seq')
- grad_proj: float32 [2, 1024, 512], P(None, 'seq')
- grad_gains_in: float32 [2, 1024], replicated
- grad_biases_in: float32 [2, 1024], replicated
- grad_gains_mid: float32 [2, 512], replicated
- grad_biases_mid: float32 [2, 512], replicated
The draws below stay inside these ranges and needn't reach their ends.
Inputs may be any that keep to these rules, and one draw needn't show every extreme that they name: `segment_ids`: never falling along a window; each interval holds 256 to 768 bins, and every window has one of the largest length; bin t lies in interval s exactly when interval_bounds[w, s] <= t < interval_bounds[w, s + 1]. `interval_bounds`: rising in each window, first entry 0 and last entry 8192.
All inputs are finite; a program needn't handle non-finite values.
Results may differ from the reference program's by a relative error of at most 0.02.
Values may be sent and summed in bfloat16 or wider, within the bound.
No kernel may reach another device: no remote copies, remote signals or barrier semaphores. Data moves between devices by JAX's collectives and lax.ppermute only.
A program may use at most 128 MiB of HBM per device.

```python
import jax
import jax.numpy as jnp
from jax import lax

CH = 1024
HALF = 512
LAYERS = 2
FIRST_DILATION = 64
SECOND_DILATION = 512
SEG_SPAN = 512
WINDOWS = 4
BINS = 8192
SEGS = 16


def interval_table(key):
    subkeys = jax.random.split(key, WINDOWS)

    def one_window(window_key):
        first_key, second_key = jax.random.split(window_key)
        pair_count = SEGS // 2
        excess = jax.random.randint(first_key, (pair_count,), 0, SEG_SPAN // 2 + 1)
        excess = jnp.where(jnp.arange(pair_count) == 0, SEG_SPAN // 2, excess)
        lengths = jnp.concatenate([SEG_SPAN + excess, SEG_SPAN - excess])
        lengths = lengths[jax.random.permutation(second_key, SEGS)]
        return jnp.concatenate([jnp.zeros((1,), jnp.int32), jnp.cumsum(lengths).astype(jnp.int32)])
    return jax.vmap(one_window)(subkeys).astype(jnp.int32)


def draw_interval_bounds(key, part):
    return interval_table(key)


def draw_segment_ids(key, part):
    boundary = interval_table(key)
    position = jnp.arange(BINS, dtype=jnp.int32)
    opened = boundary[:, None, :-1] <= position[None, :, None]
    return (jnp.sum(opened.astype(jnp.int32), axis=2) - 1).astype(jnp.int32)


def draw_activations(key, part):
    key = jax.random.fold_in(key, 11)
    first_key, second_key = jax.random.split(key, 2)
    rising = (3.0 ** (jnp.arange(BINS, dtype=jnp.float32) / BINS))[None, :, None]
    entries = jnp.clip(jax.random.normal(first_key, (WINDOWS, BINS, CH), jnp.float32), -4.0, 4.0)
    row_scale = jnp.exp(jax.random.uniform(second_key, (WINDOWS, BINS, 1), jnp.float32, -0.8, 0.8))
    values = entries * row_scale * rising
    return values.astype(jnp.bfloat16)


def strengthened(values, stream_key, source, target, blocks, factor):
    def block_of(dim):
        return (jnp.arange(values.shape[dim]) // (values.shape[dim] // blocks)).reshape((-1,) + (1,) * (values.ndim - 1 - dim))

    one_side = jax.random.permutation(stream_key, blocks)[block_of(target)]
    far = (block_of(target) + blocks // 2) % blocks
    return jnp.where((block_of(source) == one_side) | (block_of(source) == far), factor * values, values)


def levels(own_key, dims, pieces, least, high):
    def one(axis_at, parts):
        heights = jax.random.uniform(jax.random.fold_in(jax.random.fold_in(own_key, 6), axis_at), (parts,), jnp.float32, least / len(pieces), high / len(pieces))
        return jnp.repeat(jnp.exp(heights), dims[axis_at] // parts).reshape((-1,) + (1,) * (len(dims) - axis_at - 1))

    loudness = one(*pieces[0])
    for cut in pieces[1:]:
        loudness = loudness * one(*cut)
    return loudness


def centred(own_key, dims, scale, most, cuts=(), kind=jnp.bfloat16):
    factor_of = levels(own_key, dims, cuts, -0.22, 0.18) if cuts else 1.0
    values = jax.random.normal(own_key, dims, jnp.float32) * scale * factor_of
    return jnp.minimum(jnp.maximum(values, -most), most).astype(kind)


def noise_with(own_key, dims, width, most, cuts, heavy, kind=jnp.bfloat16):
    drawn = width * jax.random.normal(own_key, dims, jnp.float32)
    if cuts:
        drawn = drawn * levels(own_key, dims, cuts, -0.22, 0.18)
    return jnp.clip(strengthened(drawn, jax.random.fold_in(own_key, 3), *heavy), -most, most).astype(kind)


def setup_inputs(seed: int = 0) -> dict:
    arg_keys = jax.random.split(jax.random.key(seed), 11)
    activations = draw_activations(jax.random.fold_in(arg_keys[10], 71), 0)
    segment_ids = draw_segment_ids(jax.random.fold_in(arg_keys[10], 71), 0)
    interval_bounds = draw_interval_bounds(jax.random.fold_in(arg_keys[10], 71), 0)
    conv_weight = centred(arg_keys[3], (LAYERS, CH, 3 * HALF), (3 * CH) ** -0.5, 0.109375)
    proj_weight = centred(arg_keys[4], (LAYERS, CH, HALF), HALF ** -0.5, 0.25)
    gains_in = jnp.clip(1.0 + 0.15 * jax.random.normal(arg_keys[5], (LAYERS, CH), jnp.float32), 0.25, 1.75)
    biases_in = centred(arg_keys[6], (LAYERS, CH), 0.5, 2.5, (), jnp.float32)
    gains_mid = jnp.clip(1.0 + 0.15 * jax.random.normal(arg_keys[7], (LAYERS, HALF), jnp.float32), 0.25, 1.75)
    biases_mid = centred(arg_keys[8], (LAYERS, HALF), 0.5, 2.5, (), jnp.float32)
    cotangent = noise_with(arg_keys[9], (WINDOWS, BINS, CH), 1.0, 24.0, ((0, 2), (1, 128)), (1, 2, 128, 5.5))
    return {"activations": activations, "segment_ids": segment_ids, "interval_bounds": interval_bounds, "conv_weight": conv_weight, "proj_weight": proj_weight, "gains_in": gains_in, "biases_in": biases_in, "gains_mid": gains_mid, "biases_mid": biases_mid, "cotangent": cotangent}


EPSILON = 1e-05

def gelu_slope(values):
    return jax.jvp(lambda argument: jax.nn.gelu(argument, approximate=True), (values,), (jnp.ones_like(values),))

def batch_norm(values, norm_gain, norm_bias):
    middle_tap = lax.optimization_barrier(jnp.mean(values, axis=0))
    shifted = values - middle_tap
    spread = lax.optimization_barrier(jnp.mean(shifted * shifted, axis=0))
    factor = lax.rsqrt(spread + EPSILON)
    normed = shifted * factor
    return (normed, factor, normed * norm_gain + norm_bias)

def norm_back(upstream, normed, factor, norm_gain):
    number = upstream.shape[0]
    total_sum = lax.optimization_barrier(jnp.sum(upstream, axis=0))
    cross_sum = lax.optimization_barrier(jnp.sum(upstream * normed, axis=0))
    result = norm_gain * factor * (upstream - total_sum / number - normed * cross_sum / number)
    return (result, cross_sum, total_sum)

def shift_down(tensor, dilation):
    zeros_block = jnp.zeros_like(tensor[:, :dilation])
    return jnp.concatenate([zeros_block, tensor[:, :-dilation]], axis=1)

def shift_up(tensor, dilation):
    zeros_block = jnp.zeros_like(tensor[:, :dilation])
    return jnp.concatenate([tensor[:, dilation:], zeros_block], axis=1)

def interval_edges(segment_ids, interval_bounds):
    labels = jnp.arange(interval_bounds.shape[1] - 1, dtype=jnp.int32)
    matches = segment_ids[:, :, None] == labels[None, None, :]
    starts = lax.optimization_barrier(jnp.sum(jnp.where(matches, interval_bounds[:, None, :-1], 0), axis=2))
    finishes = lax.optimization_barrier(jnp.sum(jnp.where(matches, interval_bounds[:, None, 1:], 0), axis=2))
    return (starts, finishes)

def reference(activations, segment_ids, interval_bounds, conv_weight, proj_weight, gains_in, biases_in, gains_mid, biases_mid, cotangent):
    total_rows = WINDOWS * BINS
    dilation_list = (FIRST_DILATION, SECOND_DILATION)
    starts, finishes = interval_edges(segment_ids, interval_bounds)
    position = jnp.arange(BINS, dtype=jnp.int32)[None, :]
    stream = activations
    caches = []
    for layer_index in range(LAYERS):
        dilation = dilation_list[layer_index]
        mask_before = (starts <= position - dilation).astype(jnp.bfloat16)[:, :, None]
        mask_after = (position + dilation < finishes).astype(jnp.bfloat16)[:, :, None]
        kernel = conv_weight[layer_index]
        project = proj_weight[layer_index]
        flattened_rows = stream.reshape(total_rows, CH).astype(jnp.float32)
        normed_in, factor_in, preact_in = batch_norm(flattened_rows, gains_in[layer_index], biases_in[layer_index])
        active_in, slope_in = gelu_slope(preact_in)
        centre_taps = active_in.astype(jnp.bfloat16)
        cube = centre_taps.reshape(WINDOWS, BINS, CH)
        before_taps = (shift_down(cube, dilation) * mask_before).reshape(total_rows, CH)
        after_taps = (shift_up(cube, dilation) * mask_after).reshape(total_rows, CH)
        conv_out = jnp.dot(before_taps, kernel[:, :HALF], preferred_element_type=jnp.float32)
        conv_out = conv_out + jnp.dot(centre_taps, kernel[:, HALF:2 * HALF], preferred_element_type=jnp.float32)
        conv_out = conv_out + jnp.dot(after_taps, kernel[:, 2 * HALF:], preferred_element_type=jnp.float32)
        normed_mid, factor_mid, preact_mid = batch_norm(conv_out, gains_mid[layer_index], biases_mid[layer_index])
        middle_activation, slope_mid = gelu_slope(preact_mid)
        hidden = middle_activation.astype(jnp.bfloat16)
        branch = jnp.dot(hidden, project.T, preferred_element_type=jnp.float32)
        stream = (flattened_rows + branch).astype(jnp.bfloat16).reshape(WINDOWS, BINS, CH)
        caches.append((mask_before, mask_after, normed_in, factor_in, slope_in, centre_taps, before_taps, after_taps, normed_mid, factor_mid, slope_mid, hidden))
    grad_stream = cotangent
    kernel_grads = []
    project_grads = []
    gain_in_grads = []
    bias_in_grads = []
    gain_mid_grads = []
    bias_mid_grads = []
    for layer_index in range(LAYERS - 1, -1, -1):
        dilation = dilation_list[layer_index]
        mask_before, mask_after, normed_in, factor_in, slope_in, centre_taps, before_taps, after_taps, normed_mid, factor_mid, slope_mid, hidden = caches[layer_index]
        kernel = conv_weight[layer_index]
        project = proj_weight[layer_index]
        upstream = grad_stream.reshape(total_rows, CH)
        grad_hidden = jnp.dot(upstream, project, preferred_element_type=jnp.float32)
        grad_preact_mid = grad_hidden * slope_mid
        grad_conv_f, gain_mid_grad, bias_mid_grad = norm_back(grad_preact_mid, normed_mid, factor_mid, gains_mid[layer_index])
        grad_conv_out = grad_conv_f.astype(jnp.bfloat16)
        cube = grad_conv_out.reshape(WINDOWS, BINS, HALF)
        grad_before = (shift_down(cube, dilation) * mask_before).reshape(total_rows, HALF)
        grad_after = (shift_up(cube, dilation) * mask_after).reshape(total_rows, HALF)
        grad_taps = jnp.dot(grad_after, kernel[:, :HALF].T, preferred_element_type=jnp.float32)
        grad_taps = grad_taps + jnp.dot(grad_conv_out, kernel[:, HALF:2 * HALF].T, preferred_element_type=jnp.float32)
        grad_taps = grad_taps + jnp.dot(grad_before, kernel[:, 2 * HALF:].T, preferred_element_type=jnp.float32)
        grad_preact_in = grad_taps * slope_in
        grad_branch, gain_in_grad, entry_bias_gradient = norm_back(grad_preact_in, normed_in, factor_in, gains_in[layer_index])
        kernel_grad = jnp.concatenate([jnp.dot(before_taps.T, grad_conv_out, preferred_element_type=jnp.float32), jnp.dot(centre_taps.T, grad_conv_out, preferred_element_type=jnp.float32), jnp.dot(after_taps.T, grad_conv_out, preferred_element_type=jnp.float32)], axis=1)
        project_grad = jnp.dot(upstream.T, hidden, preferred_element_type=jnp.float32)
        grad_stream = (upstream.astype(jnp.float32) + grad_branch).astype(jnp.bfloat16).reshape(WINDOWS, BINS, CH)
        kernel_grads.append(kernel_grad)
        project_grads.append(project_grad)
        gain_in_grads.append(gain_in_grad)
        bias_in_grads.append(entry_bias_gradient)
        gain_mid_grads.append(gain_mid_grad)
        bias_mid_grads.append(bias_mid_grad)
    return (stream, grad_stream, jnp.stack(kernel_grads[::-1]), jnp.stack(project_grads[::-1]), jnp.stack(gain_in_grads[::-1]), jnp.stack(bias_in_grads[::-1]), jnp.stack(gain_mid_grads[::-1]), jnp.stack(bias_mid_grads[::-1]))
```

```python
import jax
import jax.numpy as jnp
from jax import lax
from jax.sharding import Mesh, PartitionSpec as P

LAYERS = 2
FIRST_DILATION = 64
SECOND_DILATION = 512
EPSILON = 1e-05

SIZES = {"dp": 2, "y": 4, "x": 4, "z": 8}
SEQ = ("y", "x", "z")
STAGES = (("dp", "z"), ("y", "x"))
F32 = jnp.float32
BF16 = jnp.bfloat16


def size_of(axes):
    total = 1
    for name in (axes if isinstance(axes, tuple) else (axes,)):
        total *= SIZES[name]
    return total


def shared(value, axes):
    count = size_of(axes)
    return lax.all_to_all(
        jnp.broadcast_to(value[None], (count,) + value.shape), axes, 0, 0, tiled=True
    )


def total_over_all(first, second):
    width = first.shape[0]
    both = jnp.concatenate([first, second])
    for axes in STAGES:
        both = jnp.sum(shared(both, axes), axis=0)
    return both[:width], both[width:]


def moments_over_all(values):
    rows, width = values.shape
    mean = jnp.mean(values, axis=0)
    centred = values - mean
    square = jnp.mean(centred * centred, axis=0)
    for axes in STAGES:
        parts = shared(jnp.concatenate([mean, square]), axes)
        means, squares = parts[:, :width], parts[:, width:]
        mean = jnp.mean(means, axis=0)
        offset = means - mean
        square = jnp.mean(squares + offset * offset, axis=0)
    return mean, square


def gelu_slope(values):
    return jax.jvp(
        lambda argument: jax.nn.gelu(argument, approximate=True),
        (values,),
        (jnp.ones_like(values),),
    )


def normalise(values, norm_gain, norm_bias):
    mean, spread = moments_over_all(values)
    factor = lax.rsqrt(spread + EPSILON)
    normed = (values - mean) * factor
    return (normed, factor, normed * norm_gain + norm_bias)


def normalise_back(upstream, normed, factor, norm_gain, count_all):
    total_sum, cross_sum = total_over_all(
        jnp.sum(upstream, axis=0), jnp.sum(upstream * normed, axis=0)
    )
    result = (
        norm_gain * factor * (upstream - total_sum / count_all - normed * cross_sum / count_all)
    )
    return (result, cross_sum, total_sum)


def passed_along(value, steps):
    count = size_of(SEQ)
    leading, last = (max(0, -steps), min(count, count - steps))
    return lax.ppermute(value, SEQ, [(source, source + steps) for source in range(leading, last)])


def neighbour_taps(tensor, dilation):
    local_bins = tensor.shape[1]
    device_hops = dilation // local_bins
    return passed_along(tensor, device_hops), passed_along(tensor, -device_hops)


def transposed_product(left_side, right_side):
    return lax.dot_general(
        left_side, right_side, (((1,), (1,)), ((), ())), preferred_element_type=F32
    )


def column_product(left_side, right_side):
    return lax.dot_general(
        left_side, right_side, (((0,), (0,)), ((), ())), preferred_element_type=F32
    )


def row_share(left_side, right_side):
    half = right_side.shape[1] // 2
    place = lax.axis_index("dp")
    kept = lax.dynamic_slice_in_dim(right_side, place * half, half, 1)
    given = lax.dynamic_slice_in_dim(right_side, (1 - place) * half, half, 1)
    swap = [(0, 1), (1, 0)]
    arrived = lax.ppermute(column_product(left_side, given).astype(BF16), "dp", swap)
    part = (column_product(left_side, kept) + arrived.astype(F32)).astype(BF16)
    for axes in (("y", "x"), "z"):
        count = size_of(axes)
        part = part.reshape(count, part.shape[0] // count, half)
        part = lax.all_to_all(part, axes, 0, 0, tiled=True)
        part = jnp.sum(part.astype(F32), axis=0)
        if axes != "z":
            part = part.astype(BF16)
    other = lax.ppermute(part, "dp", swap)
    lower = jnp.where(place == 0, part, other)
    upper = jnp.where(place == 0, other, part)
    return jnp.concatenate([lower, upper], axis=1)


def on_device(
    activations,
    segment_ids,
    interval_bounds,
    conv_weight,
    proj_weight,
    gains_in,
    biases_in,
    gains_mid,
    biases_mid,
    cotangent,
):
    windows, local_bins, channels = activations.shape
    hidden_width = proj_weight.shape[2]
    local_rows = windows * local_bins
    count_all = float(local_rows * size_of(("dp",) + SEQ))
    dilation_list = (FIRST_DILATION, SECOND_DILATION)
    position = lax.axis_index(SEQ) * local_bins + jnp.arange(local_bins, dtype=jnp.int32)[None, :]
    labels = jnp.arange(interval_bounds.shape[1] - 1, dtype=jnp.int32)
    matches = segment_ids[:, :, None] == labels[None, None, :]
    starts = jnp.sum(jnp.where(matches, interval_bounds[:, None, :-1], 0), axis=2)
    finishes = jnp.sum(jnp.where(matches, interval_bounds[:, None, 1:], 0), axis=2)
    stream = activations
    caches = []
    for layer_index in range(LAYERS):
        dilation = dilation_list[layer_index]
        mask_before = (starts <= position - dilation).astype(BF16)[:, :, None]
        mask_after = (position + dilation < finishes).astype(BF16)[:, :, None]
        kernel = conv_weight[layer_index]
        project = proj_weight[layer_index]
        flattened_rows = stream.reshape(local_rows, channels).astype(F32)
        normed_in, factor_in, preact_in = normalise(
            flattened_rows, gains_in[layer_index], biases_in[layer_index]
        )
        active_in, slope_in = gelu_slope(preact_in)
        centre_taps = active_in.astype(BF16)
        lower_taps, upper_taps = neighbour_taps(
            centre_taps.reshape(windows, local_bins, channels), dilation
        )
        before_taps = (lower_taps * mask_before).reshape(local_rows, channels)
        after_taps = (upper_taps * mask_after).reshape(local_rows, channels)
        conv_out = jnp.dot(
            centre_taps,
            kernel[:, hidden_width : 2 * hidden_width],
            preferred_element_type=F32,
        )
        conv_out = conv_out + jnp.dot(
            before_taps, kernel[:, :hidden_width], preferred_element_type=F32
        )
        conv_out = conv_out + jnp.dot(
            after_taps, kernel[:, 2 * hidden_width :], preferred_element_type=F32
        )
        normed_mid, factor_mid, preact_mid = normalise(
            conv_out, gains_mid[layer_index], biases_mid[layer_index]
        )
        middle_activation, slope_mid = gelu_slope(preact_mid)
        hidden = middle_activation.astype(BF16)
        branch = transposed_product(hidden, project)
        stream = (flattened_rows + branch).astype(BF16).reshape(windows, local_bins, channels)
        caches.append(
            (
                mask_before,
                mask_after,
                normed_in,
                factor_in,
                slope_in,
                centre_taps,
                normed_mid,
                factor_mid,
                slope_mid,
                hidden,
            )
        )
    grad_stream = cotangent
    kernel_grads = []
    project_grads = []
    gain_in_grads = []
    bias_in_grads = []
    gain_mid_grads = []
    bias_mid_grads = []
    for layer_index in range(LAYERS - 1, -1, -1):
        dilation = dilation_list[layer_index]
        (
            mask_before,
            mask_after,
            normed_in,
            factor_in,
            slope_in,
            centre_taps,
            normed_mid,
            factor_mid,
            slope_mid,
            hidden,
        ) = caches[layer_index]
        kernel = conv_weight[layer_index]
        project = proj_weight[layer_index]
        upstream = grad_stream.reshape(local_rows, channels)
        grad_hidden = jnp.dot(upstream, project, preferred_element_type=F32)
        project_grads.append(row_share(upstream, hidden))
        grad_preact_mid = grad_hidden * slope_mid
        grad_conv_f, gain_mid_grad, bias_mid_grad = normalise_back(
            grad_preact_mid, normed_mid, factor_mid, gains_mid[layer_index], count_all
        )
        grad_conv_out = grad_conv_f.astype(BF16)
        lower_grad, upper_grad = neighbour_taps(
            grad_conv_out.reshape(windows, local_bins, hidden_width), dilation
        )
        grad_before = (lower_grad * mask_before).reshape(local_rows, hidden_width)
        grad_after = (upper_grad * mask_after).reshape(local_rows, hidden_width)
        grad_three = jnp.concatenate([grad_after, grad_conv_out, grad_before], axis=1)
        grad_taps = transposed_product(grad_three, kernel)
        kernel_grads.append(row_share(centre_taps, grad_three))
        grad_preact_in = grad_taps * slope_in
        grad_branch, gain_in_grad, bias_in_grad = normalise_back(
            grad_preact_in, normed_in, factor_in, gains_in[layer_index], count_all
        )
        grad_stream = (
            (upstream.astype(F32) + grad_branch)
            .astype(BF16)
            .reshape(windows, local_bins, channels)
        )
        gain_in_grads.append(gain_in_grad)
        bias_in_grads.append(bias_in_grad)
        gain_mid_grads.append(gain_mid_grad)
        bias_mid_grads.append(bias_mid_grad)
    return (
        stream,
        grad_stream,
        jnp.stack(kernel_grads[::-1]),
        jnp.stack(project_grads[::-1]),
        jnp.stack(gain_in_grads[::-1]),
        jnp.stack(bias_in_grads[::-1]),
        jnp.stack(gain_mid_grads[::-1]),
        jnp.stack(bias_mid_grads[::-1]),
    )


def solution(mesh):
    sizes = tuple(SIZES.values())
    split = Mesh(mesh.devices.reshape(sizes), tuple(SIZES))
    in_specs = (
        P("dp", SEQ, None),
        P("dp", SEQ),
        P("dp", None),
        P(),
        P(),
        P(),
        P(),
        P(),
        P(),
        P("dp", SEQ, None),
    )
    out_specs = (
        P("dp", SEQ, None),
        P("dp", SEQ, None),
        P(None, SEQ, None),
        P(None, SEQ, None),
        P(),
        P(),
        P(),
        P(),
    )
    return jax.shard_map(
        on_device, mesh=split, in_specs=in_specs, out_specs=out_specs, check_vma=False
    )
```

```python
import functools

import jax
import jax.numpy as jnp
from jax import lax
from jax.experimental import pallas as pl
from jax.experimental.pallas import tpu as pltpu
from jax.sharding import Mesh, PartitionSpec as P

FIRST_DILATION = 64
SECOND_DILATION = 512
EPSILON = 1e-05
SIZES = {"dp": 2, "y": 4, "x": 4, "z": 8}
SEQ = ("y", "x", "z")
FIRST_STAGE = ("dp", "z")
SECOND_STAGE = ("y", "x")
GROUP = 16
F32 = jnp.float32
BF16 = jnp.bfloat16
ROWS, CH, HALF = 128, 1024, 512
TOTAL = 32768.0
TANH_SCALE = 0.7978845608028654
CUBE = 0.044715


def gelu(v):
    return 0.5 * v * (1.0 + jnp.tanh(TANH_SCALE * (v + CUBE * (v * v * v))))


def gelu_slope(v):
    square = v * v
    t = jnp.tanh(TANH_SCALE * (v + CUBE * (square * v)))
    half = 0.5 * (1.0 + t)
    slope = half + 0.5 * v * (1.0 - t * t) * (TANH_SCALE * (1.0 + 3.0 * CUBE * square))
    return v * half, slope


def spread_out(out, first, second):
    row = jnp.concatenate([first, second], axis=1)
    for i in range(GROUP):
        out[i] = row


def local_moments(values):
    mean = jnp.sum(values, axis=0, keepdims=True) * (1.0 / ROWS)
    centred = values - mean
    return mean, jnp.sum(centred * centred, axis=0, keepdims=True) * (1.0 / ROWS)


def merged_moments(parts):
    width = parts.shape[2] // 2
    means = [parts[i, :, :width] for i in range(GROUP)]
    mean = sum(means[1:], means[0]) * (1.0 / GROUP)
    square = jnp.zeros_like(mean)
    for i in range(GROUP):
        offset = means[i] - mean
        square = square + (parts[i, :, width:] + offset * offset)
    return mean, square * (1.0 / GROUP)


def merged_sums(parts):
    width = parts.shape[2] // 2
    total = parts[0]
    for i in range(1, GROUP):
        total = total + parts[i]
    return total[:, :width], total[:, width:]


def product(left, right):
    return jnp.dot(left, right, preferred_element_type=F32)


def product_nt(left, right):
    return lax.dot_general(left, right, (((1,), (1,)), ((), ())), preferred_element_type=F32)


def product_tn(left, right):
    return lax.dot_general(left, right, (((0,), (0,)), ((), ())), preferred_element_type=F32)


def k_first(x, out):
    spread_out(out, *local_moments(x[...].astype(F32)))


def k_merge(kind, parts, *rest):
    out = rest[-1]
    merge = merged_moments if kind == "moments" else merged_sums
    spread_out(out, *merge(parts))


def k_entry(layer, parts, x, lower, upper, masks, weight, gains, biases, taps, slope, conv, stat, out):
    mean, spread = merged_moments(parts)
    factor = lax.rsqrt(spread + EPSILON)
    gain, bias = gains[layer : layer + 1], biases[layer : layer + 1]
    active, slope_in = gelu_slope((x[...].astype(F32) - mean) * factor * gain + bias)
    slope[...] = slope_in
    centre = active.astype(BF16)
    taps[...] = centre
    stat[...] = jnp.concatenate([mean, factor], axis=0)

    def side(rows, column):
        values = gelu((rows[...].astype(F32) - mean) * factor * gain + bias)
        mask = masks[:, 2 * layer + column : 2 * layer + column + 1]
        return jnp.where(mask > 0, values, 0.0).astype(BF16)

    result = product(centre, weight[:, HALF : 2 * HALF])
    result = result + product(side(lower, 0), weight[:, :HALF])
    result = result + product(side(upper, 1), weight[:, 2 * HALF :])
    conv[...] = result
    spread_out(out, *local_moments(result))


def middle(layer, parts, conv, gains, biases, project, x):
    mean, spread = merged_moments(parts)
    factor = lax.rsqrt(spread + EPSILON)
    normed = (conv[...] - mean) * factor
    active, slope = gelu_slope(normed * gains[layer : layer + 1] + biases[layer : layer + 1])
    hidden = active.astype(BF16)
    following = (x[...].astype(F32) + product_nt(hidden, project[...])).astype(BF16)
    return factor, normed, slope, hidden, following


def k_middle(parts, conv, gains, biases, project, x, hidden, following, slope, normed, factor, out):
    factor[...], normed[...], slope[...], hidden[...], rows = middle(
        0, parts, conv, gains, biases, project, x
    )
    following[...] = rows
    spread_out(out, *local_moments(rows.astype(F32)))


def begin_backward(upstream, project, slope, normed, grad, pair, out):
    values = product(upstream, project[...]) * slope
    grad[...] = values
    pair[:, :HALF] = values.astype(BF16)
    pair[:, HALF:] = normed.astype(BF16)
    spread_out(
        out,
        jnp.sum(values, axis=0, keepdims=True),
        jnp.sum(values * normed, axis=0, keepdims=True),
    )


def k_turn(parts, conv, gains, biases, project, x, upstream, hidden, following, normed, factor, grad, pair, out):
    factor[...], rows, slope, hidden[...], following[...] = middle(
        1, parts, conv, gains, biases, project, x
    )
    normed[...] = rows
    begin_backward(upstream[...], project, slope, rows, grad, pair, out)


def k_back_middle(
    layer, parts, grad, normed, factor, lower, upper, masks, gains, weight, slope, x, stat, *rest
):
    if layer == 0:
        given_gain, given_bias, three, grad_in, gain_out, bias_out, out = rest
    else:
        three, grad_in, gain_out, bias_out, out = rest
    total, cross = merged_sums(parts)
    gain_out[0:1] = cross
    bias_out[0:1] = total
    if layer == 0:
        gain_out[1:2] = given_gain[...]
        bias_out[1:2] = given_bias[...]
    total, cross = total * (1.0 / TOTAL), cross * (1.0 / TOTAL)
    scale = gains[layer : layer + 1] * factor[...]

    def conv_grad(grads, rows):
        return scale * (grads - total - rows * cross)

    def side(pair, column):
        values = conv_grad(pair[:, :HALF].astype(F32), pair[:, HALF:].astype(F32))
        mask = masks[:, 2 * layer + column : 2 * layer + column + 1]
        return jnp.where(mask > 0, values, 0.0).astype(BF16)

    three[:, :HALF] = side(upper, 1)
    three[:, HALF : 2 * HALF] = conv_grad(grad[...], normed[...]).astype(BF16)
    three[:, 2 * HALF :] = side(lower, 0)
    values = product_nt(three[...], weight[...]) * slope[...]
    grad_in[...] = values
    normed_in = (x[...].astype(F32) - stat[0:1]) * stat[1:2]
    spread_out(
        out,
        jnp.sum(values, axis=0, keepdims=True),
        jnp.sum(values * normed_in, axis=0, keepdims=True),
    )


def back_entry(layer, parts, grad_in, x, stat, gains, upstream):
    total, cross = merged_sums(parts)
    factor = stat[1:2]
    normed = (x[...].astype(F32) - stat[0:1]) * factor
    branch = (gains[layer : layer + 1] * factor) * (
        grad_in[...] - total * (1.0 / TOTAL) - normed * (cross * (1.0 / TOTAL))
    )
    return total, cross, (upstream[...].astype(F32) + branch).astype(BF16)


def k_back_entry(
    parts, grad_in, x, stat, gains, upstream, project, slope, normed, *rest
):
    gain_out, bias_out, stream, grad, pair, out = rest
    bias_out[...], gain_out[...], rows = back_entry(1, parts, grad_in, x, stat, gains, upstream)
    stream[...] = rows
    begin_backward(rows, project, slope[...], normed[...], grad, pair, out)


def k_last(parts, grad_in, x, stat, gains, upstream, given_gain, given_bias, gain_out, bias_out, stream):
    total, cross, stream[...] = back_entry(0, parts, grad_in, x, stat, gains, upstream)
    gain_out[0:1] = cross
    gain_out[1:2] = given_gain[...]
    bias_out[0:1] = total
    bias_out[1:2] = given_bias[...]


def half_of(ref, other):
    half = ref.shape[1] // 2
    place = lax.axis_index("dp")
    place = 1 - place if other else place
    return ref[:, pl.ds(pl.multiple_of(place * half, 128), half)]


def k_give(taps, three, upstream, hidden, out):
    out[:, : 3 * HALF // 2] = product_tn(taps[...], half_of(three, True)).astype(BF16)
    out[:, 3 * HALF // 2 :] = product_tn(upstream[...], half_of(hidden, True)).astype(BF16)


def k_keep(taps, three, upstream, hidden, arrived, out):
    first = arrived[:, : 3 * HALF // 2].astype(F32)
    out[:, : 3 * HALF // 2] = (product_tn(taps[...], half_of(three, False)) + first).astype(BF16)
    second = arrived[:, 3 * HALF // 2 :].astype(F32)
    out[:, 3 * HALF // 2 :] = (product_tn(upstream[...], half_of(hidden, False)) + second).astype(BF16)


def k_gather(parts, out):
    for z in range(8):
        rows = slice(8 * z, 8 * z + 8)
        total = parts[0, rows].astype(F32)
        for i in range(1, GROUP):
            total = total + parts[i, rows].astype(F32)
        total = total.astype(BF16)
        out[z] = total
        out[8 + z] = total


def k_rows(parts_0, parts_1, kernel_out, project_out):
    cut = 3 * HALF // 2
    for layer, parts in enumerate((parts_0, parts_1)):
        for d in range(2):
            total = parts[8 * d].astype(F32)
            for z in range(1, 8):
                total = total + parts[8 * d + z].astype(F32)
            kernel_out[layer, :, d * cut : (d + 1) * cut] = total[:, :cut]
            project_out[layer, :, d * HALF // 2 : (d + 1) * HALF // 2] = total[:, cut:]


def whole(value):
    shape = value.shape
    return pl.BlockSpec(shape, lambda i: (0,) * len(shape))


def layer_of(value, layer):
    return pl.BlockSpec((None,) + value.shape[1:], lambda i: (layer, 0, 0))


def call(kernel, outs, *operands, name, layers=None, waits=(), flops=1 << 22):
    layers = layers or {}
    specs = [
        layer_of(value, layers[i]) if i in layers else whole(value)
        for i, value in enumerate(operands)
    ]
    specs += [pl.BlockSpec(memory_space=pl.ANY)] * len(waits)
    shapes = [jax.ShapeDtypeStruct(shape, dtype) for shape, dtype in outs]
    moved = sum(v.size * v.dtype.itemsize for v in list(operands) + shapes)
    return pl.pallas_call(
        kernel,
        grid=(1,),
        in_specs=specs,
        out_specs=[whole(shape) for shape in shapes],
        out_shape=shapes,
        name=name,
        cost_estimate=pl.CostEstimate(flops=flops, bytes_accessed=moved, transcendentals=0),
        compiler_params=pltpu.CompilerParams(vmem_limit_bytes=48 << 20),
    )(*operands, *waits)


def exchange(value, axes):
    return lax.all_to_all(value, axes, 0, 0, tiled=True)


def over_all(payload, kind, waits=()):
    first = exchange(payload, FIRST_STAGE)
    (merged,) = call(
        functools.partial(k_merge, kind),
        [(payload.shape, F32)],
        first,
        waits=waits,
        name="merge_" + kind,
    )
    return exchange(merged, SECOND_STAGE)


def passed_along(value, steps):
    count = 128
    leading, last = (max(0, -steps), min(count, count - steps))
    return lax.ppermute(value, SEQ, [(source, source + steps) for source in range(leading, last)])


def neighbours(rows, dilation):
    hops = dilation // 64
    return passed_along(rows, hops), passed_along(rows, -hops)


def chip_share(taps, three, upstream, hidden):
    flops = 2 * ROWS * CH * CH
    (given,) = call(
        k_give, [((CH, CH), BF16)], taps, three, upstream, hidden, name="give", flops=flops
    )
    arrived = lax.ppermute(given, "dp", [(0, 1), (1, 0)])
    (share,) = call(
        k_keep, [((CH, CH), BF16)], taps, three, upstream, hidden, arrived, name="keep", flops=flops
    )
    return exchange(share.reshape(GROUP, CH // GROUP, CH), SECOND_STAGE)


def chip_rows(parts):
    (rows,) = call(k_gather, [((GROUP, 8, CH), BF16)], parts, name="gather_rows")
    return exchange(rows, FIRST_STAGE)


def on_device(
    activations,
    segment_ids,
    interval_bounds,
    conv_weight,
    proj_weight,
    gains_in,
    biases_in,
    gains_mid,
    biases_mid,
    cotangent,
):
    windows, local_bins, channels = activations.shape
    position = lax.axis_index(SEQ) * local_bins + jnp.arange(local_bins, dtype=jnp.int32)[None, :]
    labels = jnp.arange(interval_bounds.shape[1] - 1, dtype=jnp.int32)
    matches = segment_ids[:, :, None] == labels[None, None, :]
    starts = jnp.sum(jnp.where(matches, interval_bounds[:, None, :-1], 0), axis=2)
    finishes = jnp.sum(jnp.where(matches, interval_bounds[:, None, 1:], 0), axis=2)
    masks = []
    for dilation in (FIRST_DILATION, SECOND_DILATION):
        masks.append(starts <= position - dilation)
        masks.append(position + dilation < finishes)
    masks = jnp.stack(masks, axis=2).astype(F32).reshape(ROWS, 4)

    wide, narrow = (GROUP, 1, 2 * CH), (GROUP, 1, CH)
    conv_flops = 2 * ROWS * CH * 3 * HALF
    stream_0 = activations.reshape(ROWS, CH)
    grad_2 = cotangent.reshape(ROWS, CH)

    def entry(layer, stream, parts, sides):
        return call(
            functools.partial(k_entry, layer),
            [((ROWS, CH), BF16), ((ROWS, CH), F32), ((ROWS, HALF), F32), ((2, CH), F32), (narrow, F32)],
            parts,
            stream,
            *sides,
            masks,
            conv_weight,
            gains_in,
            biases_in,
            layers={5: layer},
            name="entry",
            flops=conv_flops,
        )

    sides = neighbours(stream_0, FIRST_DILATION)
    (payload,) = call(k_first, [(wide, F32)], stream_0, name="first")
    parts = over_all(payload, "moments", sides)
    taps_0, slope_0, conv_0, stat_0, payload = entry(0, stream_0, parts, sides)
    parts = over_all(payload, "moments")
    hidden_0, stream_1, slope_mid_0, normed_0, factor_0, payload = call(
        k_middle,
        [
            ((ROWS, HALF), BF16),
            ((ROWS, CH), BF16),
            ((ROWS, HALF), F32),
            ((ROWS, HALF), F32),
            ((1, HALF), F32),
            (wide, F32),
        ],
        parts,
        conv_0,
        gains_mid,
        biases_mid,
        proj_weight,
        stream_0,
        layers={4: 0},
        name="middle",
    )
    sides = neighbours(stream_1, SECOND_DILATION)
    parts = over_all(payload, "moments", sides)
    taps_1, slope_1, conv_1, stat_1, payload = entry(1, stream_1, parts, sides)
    parts = over_all(payload, "moments")
    hidden_1, stream_2, normed_1, factor_1, grad, pair, payload = call(
        k_turn,
        [
            ((ROWS, HALF), BF16),
            ((ROWS, CH), BF16),
            ((ROWS, HALF), F32),
            ((1, HALF), F32),
            ((ROWS, HALF), F32),
            ((ROWS, CH), BF16),
            (narrow, F32),
        ],
        parts,
        conv_1,
        gains_mid,
        biases_mid,
        proj_weight,
        stream_1,
        grad_2,
        layers={4: 1},
        name="turn",
    )

    def back_middle(layer, parts, grad, normed, factor, sides, slope, stream, stat, *given):
        rows = 2 - layer
        return call(
            functools.partial(k_back_middle, layer),
            [
                ((ROWS, 3 * HALF), BF16),
                ((ROWS, CH), F32),
                ((rows, HALF), F32),
                ((rows, HALF), F32),
                (wide, F32),
            ],
            parts,
            grad,
            normed,
            factor,
            *sides,
            masks,
            gains_mid,
            conv_weight,
            slope,
            stream,
            stat,
            *given,
            layers={8: layer},
            name="back_middle",
            flops=conv_flops,
        )

    sides = neighbours(pair, SECOND_DILATION)
    parts = over_all(payload, "sums", sides)
    three_1, grad_in, gain_mid, bias_mid, payload = back_middle(
        1, parts, grad, normed_1, factor_1, sides, slope_1, stream_1, stat_1
    )
    parts = over_all(payload, "sums")
    gain_in, bias_in, grad_1, grad, pair, payload = call(
        k_back_entry,
        [
            ((1, CH), F32),
            ((1, CH), F32),
            ((ROWS, CH), BF16),
            ((ROWS, HALF), F32),
            ((ROWS, CH), BF16),
            (narrow, F32),
        ],
        parts,
        grad_in,
        stream_1,
        stat_1,
        gains_in,
        grad_2,
        proj_weight,
        slope_mid_0,
        normed_0,
        layers={6: 0},
        name="back_entry",
    )
    sides = neighbours(pair, FIRST_DILATION)
    chip_1 = chip_share(taps_1, three_1, grad_2, hidden_1)
    parts = over_all(payload, "sums", sides)
    three_0, grad_in, grad_gains_mid, grad_biases_mid, payload = back_middle(
        0, parts, grad, normed_0, factor_0, sides, slope_0, stream_0, stat_0, gain_mid, bias_mid
    )
    rows_1 = chip_rows(chip_1)
    chip_0 = chip_share(taps_0, three_0, grad_1, hidden_0)
    parts = over_all(payload, "sums", (rows_1,))
    grad_gains_in, grad_biases_in, grad_0 = call(
        k_last,
        [((2, CH), F32), ((2, CH), F32), ((ROWS, CH), BF16)],
        parts,
        grad_in,
        stream_0,
        stat_0,
        gains_in,
        grad_1,
        gain_in,
        bias_in,
        name="last",
    )
    grad_conv, grad_proj = call(
        k_rows,
        [((2, 8, 3 * HALF), F32), ((2, 8, HALF), F32)],
        chip_rows(chip_0),
        rows_1,
        name="rows",
    )
    return (
        stream_2.reshape(activations.shape),
        grad_0.reshape(activations.shape),
        grad_conv,
        grad_proj,
        grad_gains_in,
        grad_biases_in,
        grad_gains_mid,
        grad_biases_mid,
    )


def solution(mesh):
    sizes = tuple(SIZES.values())
    split = Mesh(mesh.devices.reshape(sizes), tuple(SIZES))
    bins = P("dp", SEQ, None)
    rows = P(None, SEQ, None)
    in_specs = (bins, P("dp", SEQ), P("dp", None), P(), P(), P(), P(), P(), P(), bins)
    out_specs = (bins, bins, rows, rows, P(), P(), P(), P())
    return jax.shard_map(
        on_device, mesh=split, in_specs=in_specs, out_specs=out_specs, check_vma=False
    )
```

```python
import functools

import jax
import jax.numpy as jnp
from jax import lax
from jax.experimental import pallas as pl
from jax.experimental.pallas import tpu as pltpu
from jax.sharding import Mesh, PartitionSpec as P

FIRST_DILATION = 64
SECOND_DILATION = 512
EPSILON = 1e-05
SIZES = {"dp": 2, "y": 4, "x": 4, "z": 8}
SEQ = ("y", "x", "z")
FIRST_STAGE = ("dp", "z")
SECOND_STAGE = ("y", "x")
GROUP = 16
F32 = jnp.float32
BF16 = jnp.bfloat16
ROWS, CH, HALF = 128, 1024, 512
VMEM_LIMIT = 60 << 20
TOTAL = 32768.0
TANH_SCALE = 0.7978845608028654
CUBE = 0.044715


def gelu(v):
    return 0.5 * v * (1.0 + jnp.tanh(TANH_SCALE * (v + CUBE * (v * v * v))))


def gelu_slope(v):
    square = v * v
    t = jnp.tanh(TANH_SCALE * (v + CUBE * (square * v)))
    half = 0.5 * (1.0 + t)
    slope = half + 0.5 * v * (1.0 - t * t) * (TANH_SCALE * (1.0 + 3.0 * CUBE * square))
    return v * half, slope


def spread_out(out, first, second):
    row = jnp.concatenate([first, second], axis=1)
    for i in range(GROUP):
        out[i] = row


def local_moments(values):
    mean = jnp.sum(values, axis=0, keepdims=True) * (1.0 / ROWS)
    centred = values - mean
    return mean, jnp.sum(centred * centred, axis=0, keepdims=True) * (1.0 / ROWS)


def merged_moments(parts):
    width = parts.shape[2] // 2
    means = [parts[i, :, :width] for i in range(GROUP)]
    mean = sum(means[1:], means[0]) * (1.0 / GROUP)
    square = jnp.zeros_like(mean)
    for i in range(GROUP):
        offset = means[i] - mean
        square = square + (parts[i, :, width:] + offset * offset)
    return mean, square * (1.0 / GROUP)


def merged_sums(parts):
    width = parts.shape[2] // 2
    total = parts[0]
    for i in range(1, GROUP):
        total = total + parts[i]
    return total[:, :width], total[:, width:]


def product(left, right):
    return jnp.dot(left, right, preferred_element_type=F32)


def product_nt(left, right):
    return lax.dot_general(left, right, (((1,), (1,)), ((), ())), preferred_element_type=F32)


def product_tn(left, right):
    return lax.dot_general(left, right, (((0,), (0,)), ((), ())), preferred_element_type=F32)


def k_first(x, out):
    spread_out(out, *local_moments(x[...].astype(F32)))


def k_merge(kind, parts, *rest):
    out = rest[-1]
    merge = merged_moments if kind == "moments" else merged_sums
    if out.shape[0] == 1:
        out[...] = jnp.concatenate(merge(parts), axis=1)
    else:
        spread_out(out, *merge(parts))


def k_entry(layer, parts, x, lower, upper, masks, weight, gains, biases, taps, slope, conv, stat, out):
    mean, spread = merged_moments(parts)
    factor = lax.rsqrt(spread + EPSILON)
    gain, bias = gains[layer : layer + 1], biases[layer : layer + 1]
    active, slope_in = gelu_slope((x[...].astype(F32) - mean) * factor * gain + bias)
    slope[...] = slope_in
    centre = active.astype(BF16)
    taps[...] = centre
    stat[...] = jnp.concatenate([mean, factor], axis=0)

    def side(rows, column):
        values = gelu((rows[...].astype(F32) - mean) * factor * gain + bias)
        mask = masks[:, 2 * layer + column : 2 * layer + column + 1]
        return jnp.where(mask > 0, values, 0.0).astype(BF16)

    result = product(centre, weight[:, HALF : 2 * HALF])
    result = result + product(side(lower, 0), weight[:, :HALF])
    result = result + product(side(upper, 1), weight[:, 2 * HALF :])
    conv[...] = result
    spread_out(out, *local_moments(result))


def middle(layer, parts, conv, gains, biases, project, x):
    mean, spread = merged_moments(parts)
    factor = lax.rsqrt(spread + EPSILON)
    normed = (conv[...] - mean) * factor
    active, slope = gelu_slope(normed * gains[layer : layer + 1] + biases[layer : layer + 1])
    hidden = active.astype(BF16)
    following = (x[...].astype(F32) + product_nt(hidden, project[...])).astype(BF16)
    return factor, normed, slope, hidden, following


def k_middle(parts, conv, gains, biases, project, x, hidden, following, slope, normed, factor, out):
    factor[...], normed[...], slope[...], hidden[...], rows = middle(
        0, parts, conv, gains, biases, project, x
    )
    following[...] = rows
    spread_out(out, *local_moments(rows.astype(F32)))


def begin_backward(upstream, project, slope, normed, grad, pair, out):
    values = product(upstream, project[...]) * slope
    grad[...] = values
    pair[:, :HALF] = values.astype(BF16)
    pair[:, HALF:] = normed.astype(BF16)
    spread_out(
        out,
        jnp.sum(values, axis=0, keepdims=True),
        jnp.sum(values * normed, axis=0, keepdims=True),
    )


def k_turn(parts, conv, gains, biases, project, x, upstream, hidden, following, normed, factor, grad, pair, out):
    factor[...], rows, slope, hidden[...], following[...] = middle(
        1, parts, conv, gains, biases, project, x
    )
    normed[...] = rows
    begin_backward(upstream[...], project, slope, rows, grad, pair, out)


def k_back_middle(
    layer, parts, grad, normed, factor, lower, upper, masks, gains, weight, slope, x, stat, *rest
):
    if layer == 0:
        given_gain, given_bias, _, three, grad_in, gain_out, bias_out, out = rest
    else:
        three, grad_in, gain_out, bias_out, out = rest
    total, cross = merged_sums(parts)
    gain_out[0:1] = cross
    bias_out[0:1] = total
    if layer == 0:
        gain_out[1:2] = given_gain[...]
        bias_out[1:2] = given_bias[...]
    total, cross = total * (1.0 / TOTAL), cross * (1.0 / TOTAL)
    scale = gains[layer : layer + 1] * factor[...]

    def conv_grad(grads, rows):
        return scale * (grads - total - rows * cross)

    def side(pair, column):
        values = conv_grad(pair[:, :HALF].astype(F32), pair[:, HALF:].astype(F32))
        mask = masks[:, 2 * layer + column : 2 * layer + column + 1]
        return jnp.where(mask > 0, values, 0.0).astype(BF16)

    three[:, :HALF] = side(upper, 1)
    three[:, HALF : 2 * HALF] = conv_grad(grad[...], normed[...]).astype(BF16)
    three[:, 2 * HALF :] = side(lower, 0)
    values = product_nt(three[...], weight[...]) * slope[...]
    grad_in[...] = values
    normed_in = (x[...].astype(F32) - stat[0:1]) * stat[1:2]
    spread_out(
        out,
        jnp.sum(values, axis=0, keepdims=True),
        jnp.sum(values * normed_in, axis=0, keepdims=True),
    )


def back_entry(layer, parts, grad_in, x, stat, gains, upstream):
    if layer == 0:
        total, cross = parts[:, :CH], parts[:, CH:]
    else:
        total, cross = merged_sums(parts)
    factor = stat[1:2]
    normed = (x[...].astype(F32) - stat[0:1]) * factor
    branch = (gains[layer : layer + 1] * factor) * (
        grad_in[...] - total * (1.0 / TOTAL) - normed * (cross * (1.0 / TOTAL))
    )
    return total, cross, (upstream[...].astype(F32) + branch).astype(BF16)


def k_back_entry(
    parts, grad_in, x, stat, gains, upstream, project, slope, normed, *rest
):
    gain_out, bias_out, stream, grad, pair, out = rest
    bias_out[...], gain_out[...], rows = back_entry(1, parts, grad_in, x, stat, gains, upstream)
    stream[...] = rows
    begin_backward(rows, project, slope[...], normed[...], grad, pair, out)


def k_last(parts, grad_in, x, stat, gains, upstream, given_gain, given_bias, gain_out, bias_out, stream):
    total, cross, stream[...] = back_entry(0, parts, grad_in, x, stat, gains, upstream)
    gain_out[0:1] = cross
    gain_out[1:2] = given_gain[...]
    bias_out[0:1] = total
    bias_out[1:2] = given_bias[...]


def half_of(ref, other):
    half = ref.shape[1] // 2
    place = lax.axis_index("dp")
    place = 1 - place if other else place
    return ref[:, pl.ds(pl.multiple_of(place * half, 128), half)]


def k_give(taps, three, upstream, hidden, out):
    out[:, : 3 * HALF // 2] = product_tn(taps[...], half_of(three, True)).astype(BF16)
    out[:, 3 * HALF // 2 :] = product_tn(upstream[...], half_of(hidden, True)).astype(BF16)


def k_keep(taps, three, upstream, hidden, arrived, *rest):
    out = rest[-1]
    first = arrived[:, : 3 * HALF // 2].astype(F32)
    out[:, : 3 * HALF // 2] = (product_tn(taps[...], half_of(three, False)) + first).astype(BF16)
    second = arrived[:, 3 * HALF // 2 :].astype(F32)
    out[:, 3 * HALF // 2 :] = (product_tn(upstream[...], half_of(hidden, False)) + second).astype(BF16)


def k_gather(parts, *rest):
    out = rest[-1]
    for z in range(8):
        rows = slice(8 * z, 8 * z + 8)
        total = parts[0, rows].astype(F32)
        for i in range(1, GROUP):
            total = total + parts[i, rows].astype(F32)
        total = total.astype(BF16)
        out[z] = total
        out[8 + z] = total


def k_rows(parts_0, own_1, other_1, kernel_out, project_out):
    cut, width = 3 * HALF // 2, HALF // 2
    place = lax.axis_index("dp")
    for d in range(2):
        total = parts_0[8 * d].astype(F32)
        for z in range(1, 8):
            total = total + parts_0[8 * d + z].astype(F32)
        kernel_out[0, :, d * cut : (d + 1) * cut] = total[:, :cut]
        project_out[0, :, d * width : (d + 1) * width] = total[:, cut:]
    for rows, d in ((own_1, place), (other_1, 1 - place)):
        rows = rows[...].astype(F32)
        kernel_out[1, :, pl.ds(pl.multiple_of(d * cut, 128), cut)] = rows[:, :cut]
        project_out[1, :, pl.ds(pl.multiple_of(d * width, 128), width)] = rows[:, cut:]


def whole(value):
    shape = value.shape
    return pl.BlockSpec(shape, lambda i: (0,) * len(shape))


def layer_of(value, layer):
    return pl.BlockSpec((None,) + value.shape[1:], lambda i: (layer, 0, 0))


def call(kernel, outs, *operands, name, layers=None, waits=(), flops=1 << 22):
    layers = layers or {}
    specs = [
        layer_of(value, layers[i]) if i in layers else whole(value)
        for i, value in enumerate(operands)
    ]
    specs += [pl.BlockSpec(memory_space=pl.ANY)] * len(waits)
    shapes = [jax.ShapeDtypeStruct(shape, dtype) for shape, dtype in outs]
    moved = sum(v.size * v.dtype.itemsize for v in list(operands) + shapes)
    return pl.pallas_call(
        kernel,
        grid=(1,),
        in_specs=specs,
        out_specs=[whole(shape) for shape in shapes],
        out_shape=shapes,
        name=name,
        cost_estimate=pl.CostEstimate(flops=flops, bytes_accessed=moved, transcendentals=0),
        compiler_params=pltpu.CompilerParams(vmem_limit_bytes=VMEM_LIMIT),
    )(*operands, *waits)


def exchange(value, axes):
    return lax.all_to_all(value, axes, 0, 0, tiled=True)


def over_all(payload, kind, waits=()):
    first = exchange(payload, FIRST_STAGE)
    (merged,) = call(
        functools.partial(k_merge, kind),
        [(payload.shape, F32)],
        first,
        waits=waits,
        name="merge_" + kind,
    )
    return exchange(merged, SECOND_STAGE)


def passed_along(value, steps):
    count = 128
    leading, last = (max(0, -steps), min(count, count - steps))
    return lax.ppermute(value, SEQ, [(source, source + steps) for source in range(leading, last)])


def neighbours(rows, dilation):
    hops = dilation // 64
    return passed_along(rows, hops), passed_along(rows, -hops)


def chip_share(taps, three, upstream, hidden, waits=()):
    flops = 2 * ROWS * CH * CH
    (given,) = call(
        k_give, [((CH, CH), BF16)], taps, three, upstream, hidden, name="give", flops=flops
    )
    arrived = lax.ppermute(given, "dp", [(0, 1), (1, 0)])
    (share,) = call(
        k_keep,
        [((CH, CH), BF16)],
        taps,
        three,
        upstream,
        hidden,
        arrived,
        waits=waits,
        name="keep",
        flops=flops,
    )
    return share


def swapped(value, axis, step):
    pairs = [(i, i ^ step) for i in range(SIZES[axis])]
    return lax.ppermute(value, axis, pairs)


def rows_over(share, axis):
    return lax.psum_scatter(share, axis, scatter_dimension=0, tiled=True)


def rows_at_once(share, waits):
    parts = exchange(share.reshape(GROUP, CH // GROUP, CH), SECOND_STAGE)
    (rows,) = call(k_gather, [((GROUP, 8, CH), BF16)], parts, waits=waits, name="gather_rows")
    return exchange(rows, FIRST_STAGE)


def on_device(
    activations,
    segment_ids,
    interval_bounds,
    conv_weight,
    proj_weight,
    gains_in,
    biases_in,
    gains_mid,
    biases_mid,
    cotangent,
):
    windows, local_bins, channels = activations.shape
    position = lax.axis_index(SEQ) * local_bins + jnp.arange(local_bins, dtype=jnp.int32)[None, :]
    labels = jnp.arange(interval_bounds.shape[1] - 1, dtype=jnp.int32)
    matches = segment_ids[:, :, None] == labels[None, None, :]
    starts = jnp.sum(jnp.where(matches, interval_bounds[:, None, :-1], 0), axis=2)
    finishes = jnp.sum(jnp.where(matches, interval_bounds[:, None, 1:], 0), axis=2)
    masks = []
    for dilation in (FIRST_DILATION, SECOND_DILATION):
        masks.append(starts <= position - dilation)
        masks.append(position + dilation < finishes)
    masks = jnp.stack(masks, axis=2).astype(F32).reshape(ROWS, 4)

    wide, narrow = (GROUP, 1, 2 * CH), (GROUP, 1, CH)
    conv_flops = 2 * ROWS * CH * 3 * HALF
    stream_0 = activations.reshape(ROWS, CH)
    grad_2 = cotangent.reshape(ROWS, CH)

    def entry(layer, stream, parts, sides):
        return call(
            functools.partial(k_entry, layer),
            [((ROWS, CH), BF16), ((ROWS, CH), F32), ((ROWS, HALF), F32), ((2, CH), F32), (narrow, F32)],
            parts,
            stream,
            *sides,
            masks,
            conv_weight,
            gains_in,
            biases_in,
            layers={5: layer},
            name="entry",
            flops=conv_flops,
        )

    sides = neighbours(stream_0, FIRST_DILATION)
    (payload,) = call(k_first, [(wide, F32)], stream_0, name="first")
    parts = over_all(payload, "moments", sides)
    taps_0, slope_0, conv_0, stat_0, payload = entry(0, stream_0, parts, sides)
    parts = over_all(payload, "moments")
    hidden_0, stream_1, slope_mid_0, normed_0, factor_0, payload = call(
        k_middle,
        [
            ((ROWS, HALF), BF16),
            ((ROWS, CH), BF16),
            ((ROWS, HALF), F32),
            ((ROWS, HALF), F32),
            ((1, HALF), F32),
            (wide, F32),
        ],
        parts,
        conv_0,
        gains_mid,
        biases_mid,
        proj_weight,
        stream_0,
        layers={4: 0},
        name="middle",
    )
    sides = neighbours(stream_1, SECOND_DILATION)
    parts = over_all(payload, "moments", sides)
    taps_1, slope_1, conv_1, stat_1, payload = entry(1, stream_1, parts, sides)
    parts = over_all(payload, "moments")
    hidden_1, stream_2, normed_1, factor_1, grad, pair, payload = call(
        k_turn,
        [
            ((ROWS, HALF), BF16),
            ((ROWS, CH), BF16),
            ((ROWS, HALF), F32),
            ((1, HALF), F32),
            ((ROWS, HALF), F32),
            ((ROWS, CH), BF16),
            (narrow, F32),
        ],
        parts,
        conv_1,
        gains_mid,
        biases_mid,
        proj_weight,
        stream_1,
        grad_2,
        layers={4: 1},
        name="turn",
    )

    def back_middle(
        layer, parts, grad, normed, factor, sides, slope, stream, stat, *given, waits=()
    ):
        rows = 2 - layer
        return call(
            functools.partial(k_back_middle, layer),
            [
                ((ROWS, 3 * HALF), BF16),
                ((ROWS, CH), F32),
                ((rows, HALF), F32),
                ((rows, HALF), F32),
                (wide, F32),
            ],
            parts,
            grad,
            normed,
            factor,
            *sides,
            masks,
            gains_mid,
            conv_weight,
            slope,
            stream,
            stat,
            *given,
            layers={8: layer},
            waits=waits,
            name="back_middle",
            flops=conv_flops,
        )

    sides = neighbours(pair, SECOND_DILATION)
    parts = over_all(payload, "sums", sides)
    three_1, grad_in, gain_mid, bias_mid, payload = back_middle(
        1, parts, grad, normed_1, factor_1, sides, slope_1, stream_1, stat_1
    )
    parts = over_all(payload, "sums")
    gain_in, bias_in, grad_1, grad, pair, payload = call(
        k_back_entry,
        [
            ((1, CH), F32),
            ((1, CH), F32),
            ((ROWS, CH), BF16),
            ((ROWS, HALF), F32),
            ((ROWS, CH), BF16),
            (narrow, F32),
        ],
        parts,
        grad_in,
        stream_1,
        stat_1,
        gains_in,
        grad_2,
        proj_weight,
        slope_mid_0,
        normed_0,
        layers={6: 0},
        name="back_entry",
    )
    sides = neighbours(pair, FIRST_DILATION)
    rows_1 = rows_over(chip_share(taps_1, three_1, grad_2, hidden_1), "y")
    parts = over_all(payload, "sums", sides)
    three_0, grad_in, grad_gains_mid, grad_biases_mid, payload = back_middle(
        0,
        parts,
        grad,
        normed_0,
        factor_0,
        sides,
        slope_0,
        stream_0,
        stat_0,
        gain_mid,
        bias_mid,
        waits=(rows_1,),
    )
    rows_1 = rows_over(rows_1, "x")
    (sums,) = call(
        functools.partial(k_merge, "sums"),
        [((1, 2 * CH), F32)],
        exchange(payload, FIRST_STAGE),
        name="merge_sums",
    )
    chip_0 = chip_share(taps_0, three_0, grad_1, hidden_0, (sums, rows_1))
    rows_1 = rows_over(rows_1, "z")
    for axis in ("x", "y"):
        for step in (1, 2):
            sums = sums + swapped(sums, axis, step)
    grad_gains_in, grad_biases_in, grad_0 = call(
        k_last,
        [((2, CH), F32), ((2, CH), F32), ((ROWS, CH), BF16)],
        sums,
        grad_in,
        stream_0,
        stat_0,
        gains_in,
        grad_1,
        gain_in,
        bias_in,
        name="last",
    )
    grad_conv, grad_proj = call(
        k_rows,
        [((2, 8, 3 * HALF), F32), ((2, 8, HALF), F32)],
        rows_at_once(chip_0, (sums, rows_1)),
        rows_1,
        swapped(rows_1, "dp", 1),
        name="rows",
    )
    return (
        stream_2.reshape(activations.shape),
        grad_0.reshape(activations.shape),
        grad_conv,
        grad_proj,
        grad_gains_in,
        grad_biases_in,
        grad_gains_mid,
        grad_biases_mid,
    )


def solution(mesh):
    sizes = tuple(SIZES.values())
    split = Mesh(mesh.devices.reshape(sizes), tuple(SIZES))
    bins = P("dp", SEQ, None)
    rows = P(None, SEQ, None)
    in_specs = (bins, P("dp", SEQ), P("dp", None), P(), P(), P(), P(), P(), P(), bins)
    out_specs = (bins, bins, rows, rows, P(), P(), P(), P())
    return jax.shard_map(
        on_device, mesh=split, in_specs=in_specs, out_specs=out_specs, check_vma=False
    )
```

```python
import functools

import jax
import jax.numpy as jnp
from jax import lax
from jax.experimental import pallas as pl
from jax.experimental.pallas import tpu as pltpu
from jax.sharding import Mesh, PartitionSpec as P

FIRST_DILATION = 64
SECOND_DILATION = 512
EPSILON = 1e-05
SIZES = {"dp": 2, "y": 4, "x": 4, "z": 8}
SEQ = ("y", "x", "z")
FIRST_STAGE = ("dp", "z")
SECOND_STAGE = ("y", "x")
GROUP = 16
F32 = jnp.float32
BF16 = jnp.bfloat16
ROWS, CH, HALF = 128, 1024, 512
VMEM_LIMIT = 32 << 20
TOTAL = 32768.0
TANH_SCALE = 0.7978845608028654
CUBE = 0.044715


def gelu(v):
    return 0.5 * v * (1.0 + jnp.tanh(TANH_SCALE * (v + CUBE * (v * v * v))))


def gelu_slope(v):
    square = v * v
    t = jnp.tanh(TANH_SCALE * (v + CUBE * (square * v)))
    half = 0.5 * (1.0 + t)
    slope = half + 0.5 * v * (1.0 - t * t) * (TANH_SCALE * (1.0 + 3.0 * CUBE * square))
    return v * half, slope


def spread_out(out, first, second):
    row = jnp.concatenate([first, second], axis=1)
    for i in range(GROUP):
        out[i] = row


def local_moments(values):
    mean = jnp.sum(values, axis=0, keepdims=True) * (1.0 / ROWS)
    centred = values - mean
    return mean, jnp.sum(centred * centred, axis=0, keepdims=True) * (1.0 / ROWS)


def merged_moments(parts):
    width = parts.shape[2] // 2
    means = [parts[i, :, :width] for i in range(GROUP)]
    mean = sum(means[1:], means[0]) * (1.0 / GROUP)
    square = jnp.zeros_like(mean)
    for i in range(GROUP):
        offset = means[i] - mean
        square = square + (parts[i, :, width:] + offset * offset)
    return mean, square * (1.0 / GROUP)


def merged_sums(parts):
    width = parts.shape[2] // 2
    total = parts[0]
    for i in range(1, GROUP):
        total = total + parts[i]
    return total[:, :width], total[:, width:]


def product(left, right):
    return jnp.dot(left, right, preferred_element_type=F32)


def product_nt(left, right):
    return lax.dot_general(left, right, (((1,), (1,)), ((), ())), preferred_element_type=F32)


def product_tn(left, right):
    return lax.dot_general(left, right, (((0,), (0,)), ((), ())), preferred_element_type=F32)


def k_first(x, out):
    spread_out(out, *local_moments(x[...].astype(F32)))


def k_merge(kind, parts, *rest):
    out = rest[-1]
    merge = merged_moments if kind == "moments" else merged_sums
    if out.shape[0] == 1:
        out[...] = jnp.concatenate(merge(parts), axis=1)
    else:
        spread_out(out, *merge(parts))


def k_entry(layer, parts, x, lower, upper, masks, weight, gains, biases, taps, slope, conv, stat, out):
    mean, spread = merged_moments(parts)
    factor = lax.rsqrt(spread + EPSILON)
    gain, bias = gains[layer : layer + 1], biases[layer : layer + 1]
    active, slope_in = gelu_slope((x[...].astype(F32) - mean) * factor * gain + bias)
    slope[...] = slope_in
    centre = active.astype(BF16)
    taps[...] = centre
    stat[...] = jnp.concatenate([mean, factor], axis=0)

    def side(rows, column):
        values = gelu((rows[...].astype(F32) - mean) * factor * gain + bias)
        mask = masks[:, 2 * layer + column : 2 * layer + column + 1]
        return jnp.where(mask > 0, values, 0.0).astype(BF16)

    result = product(centre, weight[:, HALF : 2 * HALF])
    result = result + product(side(lower, 0), weight[:, :HALF])
    result = result + product(side(upper, 1), weight[:, 2 * HALF :])
    conv[...] = result
    spread_out(out, *local_moments(result))


def middle(layer, parts, conv, gains, biases, project, x):
    mean, spread = merged_moments(parts)
    factor = lax.rsqrt(spread + EPSILON)
    normed = (conv[...] - mean) * factor
    active, slope = gelu_slope(normed * gains[layer : layer + 1] + biases[layer : layer + 1])
    hidden = active.astype(BF16)
    following = (x[...].astype(F32) + product_nt(hidden, project[...])).astype(BF16)
    return factor, normed, slope, hidden, following


def k_middle(
    parts, conv, gains, biases, project, x, hidden, following, kept, slope, normed, factor, out
):
    factor[...], normed[...], slope[...], hidden[...], rows = middle(
        0, parts, conv, gains, biases, project, x
    )
    following[...] = rows
    kept[...] = rows
    spread_out(out, *local_moments(rows.astype(F32)))


def begin_backward(upstream, project, slope, normed, grad, pair, out):
    values = product(upstream, project[...]) * slope
    grad[...] = values
    pair[:, :HALF] = values.astype(BF16)
    pair[:, HALF:] = normed.astype(BF16)
    spread_out(
        out,
        jnp.sum(values, axis=0, keepdims=True),
        jnp.sum(values * normed, axis=0, keepdims=True),
    )


def k_turn(parts, conv, gains, biases, project, x, upstream, hidden, following, normed, factor, grad, pair, out):
    factor[...], rows, slope, hidden[...], following[...] = middle(
        1, parts, conv, gains, biases, project, x
    )
    normed[...] = rows
    begin_backward(upstream[...], project, slope, rows, grad, pair, out)


def k_back_middle(
    layer, parts, grad, normed, factor, lower, upper, masks, gains, weight, slope, x, stat, *rest
):
    if layer == 0:
        given_gain, given_bias, three, grad_in, gain_out, bias_out, out = rest
    else:
        three, grad_in, gain_out, bias_out, out = rest
    total, cross = merged_sums(parts)
    gain_out[0:1] = cross
    bias_out[0:1] = total
    if layer == 0:
        gain_out[1:2] = given_gain[...]
        bias_out[1:2] = given_bias[...]
    total, cross = total * (1.0 / TOTAL), cross * (1.0 / TOTAL)
    scale = gains[layer : layer + 1] * factor[...]

    def conv_grad(grads, rows):
        return scale * (grads - total - rows * cross)

    def side(pair, column):
        values = conv_grad(pair[:, :HALF].astype(F32), pair[:, HALF:].astype(F32))
        mask = masks[:, 2 * layer + column : 2 * layer + column + 1]
        return jnp.where(mask > 0, values, 0.0).astype(BF16)

    three[:, :HALF] = side(upper, 1)
    three[:, HALF : 2 * HALF] = conv_grad(grad[...], normed[...]).astype(BF16)
    three[:, 2 * HALF :] = side(lower, 0)
    values = product_nt(three[...], weight[...]) * slope[...]
    grad_in[...] = values
    normed_in = (x[...].astype(F32) - stat[0:1]) * stat[1:2]
    spread_out(
        out,
        jnp.sum(values, axis=0, keepdims=True),
        jnp.sum(values * normed_in, axis=0, keepdims=True),
    )


def back_entry(layer, parts, grad_in, x, stat, gains, upstream):
    if layer == 0:
        total, cross = parts[:, :CH], parts[:, CH:]
    else:
        total, cross = merged_sums(parts)
    factor = stat[1:2]
    normed = (x[...].astype(F32) - stat[0:1]) * factor
    branch = (gains[layer : layer + 1] * factor) * (
        grad_in[...] - total * (1.0 / TOTAL) - normed * (cross * (1.0 / TOTAL))
    )
    return total, cross, (upstream[...].astype(F32) + branch).astype(BF16)


def k_back_entry(
    parts, grad_in, x, stat, gains, upstream, project, slope, normed, *rest
):
    gain_out, bias_out, stream, grad, pair, out = rest
    bias_out[...], gain_out[...], rows = back_entry(1, parts, grad_in, x, stat, gains, upstream)
    stream[...] = rows
    begin_backward(rows, project, slope[...], normed[...], grad, pair, out)


def k_last(parts, grad_in, x, stat, gains, upstream, given_gain, given_bias, gain_out, bias_out, stream):
    total, cross, stream[...] = back_entry(0, parts, grad_in, x, stat, gains, upstream)
    gain_out[0:1] = cross
    gain_out[1:2] = given_gain[...]
    bias_out[0:1] = total
    bias_out[1:2] = given_bias[...]


def half_of(ref, other):
    half = ref.shape[1] // 2
    place = lax.axis_index("dp")
    place = 1 - place if other else place
    return ref[:, pl.ds(pl.multiple_of(place * half, 128), half)]


def k_give(*refs):
    out, first = refs[-1], 0
    for left, right in zip(refs[0:-1:2], refs[1:-1:2]):
        width = right.shape[1] // 2
        out[:, first : first + width] = product_tn(left[...], half_of(right, True)).astype(BF16)
        first += width


def k_keep(pairs, arrived, *refs):
    out, first = refs[-1], 0
    for i in range(pairs):
        left, right = refs[2 * i], refs[2 * i + 1]
        width = right.shape[1] // 2
        other = arrived[:, first : first + width].astype(F32)
        mine = product_tn(left[...], half_of(right, False))
        out[:, first : first + width] = (mine + other).astype(BF16)
        first += width


def k_gather(parts, other, *rest):
    out = rest[-1]
    for z in range(8):
        rows = slice(8 * z, 8 * z + 8)
        total = parts[0, rows].astype(F32)
        for i in range(1, GROUP):
            total = total + parts[i, rows].astype(F32)
        whole_row = jnp.concatenate([total.astype(BF16), other[rows, :]], axis=1)
        out[z] = whole_row
        out[8 + z] = whole_row


def k_rows(parts, kernel_out, project_out):
    cut, width = 3 * HALF // 2, HALF // 2
    for d in range(2):
        total = parts[8 * d].astype(F32)
        for z in range(1, 8):
            total = total + parts[8 * d + z].astype(F32)
        for layer in range(2):
            first = layer * CH
            kernel_out[layer, :, d * cut : (d + 1) * cut] = total[:, first : first + cut]
            project_out[layer, :, d * width : (d + 1) * width] = total[:, first + cut : first + CH]


def k_pass(value, out):
    out[...] = value[...]


def whole(value):
    shape = value.shape
    return pl.BlockSpec(shape, lambda i: (0,) * len(shape))


def in_memory(value):
    return pltpu.with_memory_space_constraint(value, pltpu.HBM)


def staged(kernel, counts, loaded, stored):
    n_in, n_waits, n_out = counts

    def body(*refs):
        ins, outs = list(refs[:n_in]), list(refs[n_in + n_waits : n_in + n_waits + n_out])
        scratch = list(refs[n_in + n_waits + n_out :])
        sems, copies, results = scratch.pop(), [], []
        for place, (i, layer) in enumerate(loaded):
            source = ins[i] if layer is None else ins[i].at[layer]
            ins[i] = scratch.pop(0)
            copies.append(pltpu.make_async_copy(source, ins[i], sems.at[place]))
            copies[-1].start()
        for place, i in enumerate(stored):
            target, outs[i] = outs[i], scratch.pop(0)
            results.append(
                pltpu.make_async_copy(outs[i], target, sems.at[len(loaded) + place])
            )
        for copy in copies:
            copy.wait()
        kernel(*ins, *outs)
        for copy in results:
            copy.start()
        for copy in results:
            copy.wait()

    return body


def call(kernel, outs, *operands, name, loaded=(), stored=(), layers=None, waits=(), held=(), flops=1 << 22):
    layers = layers or {}
    in_hbm = pl.BlockSpec(memory_space=pltpu.HBM)
    specs = [in_hbm if i in loaded else whole(value) for i, value in enumerate(operands)]
    specs += [pl.BlockSpec(memory_space=pl.ANY)] * len(waits) + [in_hbm] * len(held)
    shapes = [jax.ShapeDtypeStruct(shape, dtype) for shape, dtype in outs]
    moved = sum(v.size * v.dtype.itemsize for v in list(operands) + shapes)
    scratch = []
    for i in loaded:
        shape = operands[i].shape
        scratch.append(pltpu.VMEM(shape[1:] if i in layers else shape, operands[i].dtype))
    scratch += [pltpu.VMEM(*outs[i]) for i in stored]
    scratch.append(pltpu.SemaphoreType.DMA((max(1, len(loaded) + len(stored)),)))
    body = staged(
        kernel,
        (len(operands), len(waits) + len(held), len(outs)),
        [(i, layers.get(i)) for i in loaded],
        stored,
    )
    return pl.pallas_call(
        body,
        grid=(1,),
        in_specs=specs,
        out_specs=[in_hbm if i in stored else whole(shape) for i, shape in enumerate(shapes)],
        out_shape=[
            pltpu.HBM(shape.shape, shape.dtype) if i in stored else shape
            for i, shape in enumerate(shapes)
        ],
        scratch_shapes=scratch,
        name=name,
        cost_estimate=pl.CostEstimate(flops=flops, bytes_accessed=moved, transcendentals=0),
        compiler_params=pltpu.CompilerParams(vmem_limit_bytes=VMEM_LIMIT),
    )(
        *[in_memory(value) if i in loaded else value for i, value in enumerate(operands)],
        *waits,
        *[in_memory(value) for value in held],
    )


def exchange(value, axes):
    return lax.all_to_all(value, axes, 0, 0, tiled=True)


def over_all(payload, kind, waits=(), held=()):
    first = exchange(payload, FIRST_STAGE)
    (merged,) = call(
        functools.partial(k_merge, kind),
        [(payload.shape, F32)],
        first,
        waits=waits,
        held=held,
        name="merge_" + kind,
    )
    return exchange(merged, SECOND_STAGE), merged


def passed_along(value, steps):
    count = 128
    leading, last = (max(0, -steps), min(count, count - steps))
    return lax.ppermute(value, SEQ, [(source, source + steps) for source in range(leading, last)])


def neighbours(rows, dilation):
    hops = dilation // 64
    return passed_along(rows, hops), passed_along(rows, -hops)


def chip_share(*pairs, waits=(), waits_first=(), held=()):
    operands = [value for pair in pairs for value in pair]
    width = sum(right.shape[1] for _, right in pairs) // 2
    shape = [((CH, width), BF16)]
    flops = 2 * ROWS * CH * width
    count = len(operands)
    (given,) = call(
        k_give,
        shape,
        *operands,
        loaded=tuple(range(count)),
        waits=waits_first,
        name="give",
        flops=flops,
    )
    arrived = swapped(given, "dp", 1)
    (share,) = call(
        functools.partial(k_keep, len(pairs)),
        shape,
        arrived,
        *operands,
        loaded=tuple(range(1, count + 1)),
        stored=(0,),
        waits=waits,
        held=held,
        name="keep",
        flops=flops,
    )
    return share


def swapped(value, axis, step):
    pairs = [(i, i ^ step) for i in range(SIZES[axis])]
    return lax.ppermute(value, axis, pairs)


def rows_over(share, axis):
    return lax.psum_scatter(share, axis, scatter_dimension=0, tiled=True)


def on_device(
    activations,
    segment_ids,
    interval_bounds,
    conv_weight,
    proj_weight,
    gains_in,
    biases_in,
    gains_mid,
    biases_mid,
    cotangent,
):
    windows, local_bins, channels = activations.shape
    position = lax.axis_index(SEQ) * local_bins + jnp.arange(local_bins, dtype=jnp.int32)[None, :]
    labels = jnp.arange(interval_bounds.shape[1] - 1, dtype=jnp.int32)
    matches = segment_ids[:, :, None] == labels[None, None, :]
    starts = jnp.sum(jnp.where(matches, interval_bounds[:, None, :-1], 0), axis=2)
    finishes = jnp.sum(jnp.where(matches, interval_bounds[:, None, 1:], 0), axis=2)
    masks = []
    for dilation in (FIRST_DILATION, SECOND_DILATION):
        masks.append(starts <= position - dilation)
        masks.append(position + dilation < finishes)
    masks = jnp.stack(masks, axis=2).astype(F32).reshape(ROWS, 4)

    wide, narrow = (GROUP, 1, 2 * CH), (GROUP, 1, CH)
    conv_flops = 2 * ROWS * CH * 3 * HALF
    stream_0 = activations.reshape(ROWS, CH)
    grad_2 = cotangent.reshape(ROWS, CH)

    def entry(layer, stream, parts, sides):
        return call(
            functools.partial(k_entry, layer),
            [((ROWS, CH), BF16), ((ROWS, CH), F32), ((ROWS, HALF), F32), ((2, CH), F32), (narrow, F32)],
            parts,
            stream,
            *sides,
            masks,
            conv_weight,
            gains_in,
            biases_in,
            loaded=(5, 6, 7) if layer else (1, 5, 6, 7),
            stored=(0, 1, 3),
            layers={5: layer},
            name="entry",
            flops=conv_flops,
        )

    sides = neighbours(stream_0, FIRST_DILATION)
    (payload,) = call(k_first, [(wide, F32)], stream_0, loaded=(0,), name="first")
    parts, _ = over_all(payload, "moments", sides)
    taps_0, slope_0, conv_0, stat_0, payload = entry(0, stream_0, parts, sides)
    parts, _ = over_all(payload, "moments")
    hidden_0, stream_1, kept_1, slope_mid_0, normed_0, factor_0, payload = call(
        k_middle,
        [
            ((ROWS, HALF), BF16),
            ((ROWS, CH), BF16),
            ((ROWS, CH), BF16),
            ((ROWS, HALF), F32),
            ((ROWS, HALF), F32),
            ((1, HALF), F32),
            (wide, F32),
        ],
        parts,
        conv_0,
        gains_mid,
        biases_mid,
        proj_weight,
        stream_0,
        loaded=(2, 3, 4, 5),
        stored=(0, 2, 3, 4, 5),
        layers={4: 0},
        name="middle",
    )
    sides = neighbours(stream_1, SECOND_DILATION)
    parts, _ = over_all(payload, "moments", sides)
    taps_1, slope_1, conv_1, stat_1, payload = entry(1, stream_1, parts, sides)
    parts, _ = over_all(payload, "moments")
    hidden_1, stream_2, normed_1, factor_1, grad, pair, payload = call(
        k_turn,
        [
            ((ROWS, HALF), BF16),
            ((ROWS, CH), BF16),
            ((ROWS, HALF), F32),
            ((1, HALF), F32),
            ((ROWS, HALF), F32),
            ((ROWS, CH), BF16),
            (narrow, F32),
        ],
        parts,
        conv_1,
        gains_mid,
        biases_mid,
        proj_weight,
        kept_1,
        grad_2,
        loaded=(2, 3, 4, 5, 6),
        stored=(0, 1),
        layers={4: 1},
        name="turn",
    )

    def back_middle(
        layer, parts, grad, normed, factor, sides, slope, stream, stat, *given, held=()
    ):
        rows = 2 - layer
        return call(
            functools.partial(k_back_middle, layer),
            [
                ((ROWS, 3 * HALF), BF16),
                ((ROWS, CH), F32),
                ((rows, HALF), F32),
                ((rows, HALF), F32),
                (wide, F32),
            ],
            parts,
            grad,
            normed,
            factor,
            *sides,
            masks,
            gains_mid,
            conv_weight,
            slope,
            stream,
            stat,
            *given,
            loaded=(7, 8, 9, 10, 11) if layer else (2, 3, 7, 8, 9, 10, 11, 12, 13),
            stored=(0, 2, 3),
            layers={8: layer},
            held=held,
            name="back_middle",
            flops=conv_flops,
        )

    sides = neighbours(pair, SECOND_DILATION)
    parts, _ = over_all(payload, "sums", sides)
    three_1, grad_in, gain_mid, bias_mid, payload = back_middle(
        1, parts, grad, normed_1, factor_1, sides, slope_1, kept_1, stat_1
    )
    parts, merged = over_all(payload, "sums")
    share_1 = chip_share((taps_1, three_1), (grad_2, hidden_1), waits_first=(merged,))
    gain_in, bias_in, grad_1, grad, pair, payload = call(
        k_back_entry,
        [
            ((1, CH), F32),
            ((1, CH), F32),
            ((ROWS, CH), BF16),
            ((ROWS, HALF), F32),
            ((ROWS, CH), BF16),
            (narrow, F32),
        ],
        parts,
        grad_in,
        kept_1,
        stat_1,
        gains_in,
        grad_2,
        proj_weight,
        slope_mid_0,
        normed_0,
        loaded=(2, 3, 4, 5, 6, 7, 8),
        stored=(0, 1, 2),
        layers={6: 0},
        name="back_entry",
    )
    sides = neighbours(pair, FIRST_DILATION)
    parts, _ = over_all(payload, "sums", sides, (share_1,))
    rows_1 = rows_over(share_1, "y")
    three_0, grad_in, grad_gains_mid, grad_biases_mid, payload = back_middle(
        0,
        parts,
        grad,
        normed_0,
        factor_0,
        sides,
        slope_0,
        stream_0,
        stat_0,
        gain_mid,
        bias_mid,
    )
    (sums,) = call(
        functools.partial(k_merge, "sums"),
        [((1, 2 * CH), F32)],
        exchange(payload, FIRST_STAGE),
        name="merge_sums",
    )
    (rows_1,) = call(
        k_pass,
        [(rows_1.shape, BF16)],
        rows_1,
        loaded=(0,),
        stored=(0,),
        waits=(sums,),
        name="pass",
    )
    share_0 = chip_share((taps_0, three_0), (grad_1, hidden_0), held=(rows_1,))
    rows_1 = rows_over(rows_1, "x")
    share_0 = exchange(share_0.reshape(GROUP, CH // GROUP, CH), SECOND_STAGE)
    for axis in ("x", "y"):
        for step in (1, 2):
            sums = sums + swapped(sums, axis, step)
    grad_gains_in, grad_biases_in, grad_0 = call(
        k_last,
        [((2, CH), F32), ((2, CH), F32), ((ROWS, CH), BF16)],
        sums,
        grad_in,
        stream_0,
        stat_0,
        gains_in,
        grad_1,
        gain_in,
        bias_in,
        loaded=(2, 3, 4, 5, 6, 7),
        stored=(0, 1, 2),
        name="last",
    )
    (rows,) = call(
        k_gather,
        [((GROUP, 8, 2 * CH), BF16)],
        share_0,
        rows_1,
        loaded=(1,),
        waits=(sums,),
        name="gather_rows",
    )
    grad_conv, grad_proj = call(
        k_rows,
        [((2, 8, 3 * HALF), F32), ((2, 8, HALF), F32)],
        exchange(rows, FIRST_STAGE),
        stored=(0, 1),
        name="rows",
    )
    return (
        stream_2.reshape(activations.shape),
        grad_0.reshape(activations.shape),
        grad_conv,
        grad_proj,
        grad_gains_in,
        grad_biases_in,
        grad_gains_mid,
        grad_biases_mid,
    )


def solution(mesh):
    sizes = tuple(SIZES.values())
    split = Mesh(mesh.devices.reshape(sizes), tuple(SIZES))
    bins = P("dp", SEQ, None)
    rows = P(None, SEQ, None)
    in_specs = (bins, P("dp", SEQ), P("dp", None), P(), P(), P(), P(), P(), P(), bins)
    out_specs = (bins, bins, rows, rows, P(), P(), P(), P())
    return jax.shard_map(
        on_device, mesh=split, in_specs=in_specs, out_specs=out_specs, check_vma=False
    )
```

```python
import functools

import jax
import jax.numpy as jnp
from jax import lax
from jax.experimental import pallas as pl
from jax.experimental.pallas import tpu as pltpu
from jax.sharding import Mesh, PartitionSpec as P

FIRST_DILATION = 64
SECOND_DILATION = 512
EPSILON = 1e-05
SIZES = {"dp": 2, "y": 4, "x": 4, "z": 8}
SEQ = ("y", "x", "z")
FIRST_STAGE = ("dp", "z")
SECOND_STAGE = ("y", "x")
GROUP = 16
F32 = jnp.float32
BF16 = jnp.bfloat16
ROWS, CH, HALF = 128, 1024, 512
VMEM_LIMIT = 32 << 20
TOTAL = 32768.0
TANH_SCALE = 0.7978845608028654
CUBE = 0.044715


def gelu(v):
    return 0.5 * v * (1.0 + jnp.tanh(TANH_SCALE * (v + CUBE * (v * v * v))))


def gelu_slope(v):
    square = v * v
    t = jnp.tanh(TANH_SCALE * (v + CUBE * (square * v)))
    half = 0.5 * (1.0 + t)
    slope = half + 0.5 * v * (1.0 - t * t) * (TANH_SCALE * (1.0 + 3.0 * CUBE * square))
    return v * half, slope


def spread_out(out, first, second):
    row = jnp.concatenate([first, second], axis=1)
    for i in range(GROUP):
        out[i] = row


def local_moments(values):
    mean = jnp.sum(values, axis=0, keepdims=True) * (1.0 / ROWS)
    centred = values - mean
    return mean, jnp.sum(centred * centred, axis=0, keepdims=True) * (1.0 / ROWS)


def merged_moments(parts):
    width = parts.shape[2] // 2
    means = [parts[i, :, :width] for i in range(GROUP)]
    mean = sum(means[1:], means[0]) * (1.0 / GROUP)
    square = jnp.zeros_like(mean)
    for i in range(GROUP):
        offset = means[i] - mean
        square = square + (parts[i, :, width:] + offset * offset)
    return mean, square * (1.0 / GROUP)


def merged_sums(parts):
    width = parts.shape[2] // 2
    total = parts[0]
    for i in range(1, GROUP):
        total = total + parts[i]
    return total[:, :width], total[:, width:]


def product(left, right):
    return jnp.dot(left, right, preferred_element_type=F32)


def product_nt(left, right):
    return lax.dot_general(left, right, (((1,), (1,)), ((), ())), preferred_element_type=F32)


def product_tn(left, right):
    return lax.dot_general(left, right, (((0,), (0,)), ((), ())), preferred_element_type=F32)


def k_first(x, out):
    spread_out(out, *local_moments(x[...].astype(F32)))


def k_merge(kind, parts, *rest):
    out = rest[-1]
    merge = merged_moments if kind == "moments" else merged_sums
    if out.shape[0] == 1:
        out[...] = jnp.concatenate(merge(parts), axis=1)
    else:
        spread_out(out, *merge(parts))


def k_entry(layer, parts, x, lower, upper, masks, weight, gains, biases, taps, slope, conv, stat, out):
    mean, spread = merged_moments(parts)
    factor = lax.rsqrt(spread + EPSILON)
    gain, bias = gains[layer : layer + 1], biases[layer : layer + 1]
    active, slope_in = gelu_slope((x[...].astype(F32) - mean) * factor * gain + bias)
    slope[...] = slope_in
    centre = active.astype(BF16)
    taps[...] = centre
    stat[...] = jnp.concatenate([mean, factor], axis=0)

    def side(rows, column):
        values = gelu((rows[...].astype(F32) - mean) * factor * gain + bias)
        mask = masks[:, 2 * layer + column : 2 * layer + column + 1]
        return jnp.where(mask > 0, values, 0.0).astype(BF16)

    result = product(centre, weight[:, HALF : 2 * HALF])
    result = result + product(side(lower, 0), weight[:, :HALF])
    result = result + product(side(upper, 1), weight[:, 2 * HALF :])
    conv[...] = result
    spread_out(out, *local_moments(result))


def middle(layer, parts, conv, gains, biases, project, x):
    mean, spread = merged_moments(parts)
    factor = lax.rsqrt(spread + EPSILON)
    normed = (conv[...] - mean) * factor
    active, slope = gelu_slope(normed * gains[layer : layer + 1] + biases[layer : layer + 1])
    hidden = active.astype(BF16)
    following = (x[...].astype(F32) + product_nt(hidden, project[...])).astype(BF16)
    return factor, normed, slope, hidden, following


def k_middle(
    parts, conv, gains, biases, project, x, hidden, following, kept, slope, normed, factor, out
):
    factor[...], normed[...], slope[...], hidden[...], rows = middle(
        0, parts, conv, gains, biases, project, x
    )
    following[...] = rows
    kept[...] = rows
    spread_out(out, *local_moments(rows.astype(F32)))


def begin_backward(upstream, project, slope, normed, grad, pair, out):
    values = product(upstream, project[...]) * slope
    grad[...] = values
    pair[:, :HALF] = values.astype(BF16)
    pair[:, HALF:] = normed.astype(BF16)
    spread_out(
        out,
        jnp.sum(values, axis=0, keepdims=True),
        jnp.sum(values * normed, axis=0, keepdims=True),
    )


def k_turn(parts, conv, gains, biases, project, x, upstream, hidden, following, normed, factor, grad, pair, out):
    factor[...], rows, slope, hidden[...], following[...] = middle(
        1, parts, conv, gains, biases, project, x
    )
    normed[...] = rows
    begin_backward(upstream[...], project, slope, rows, grad, pair, out)


def k_back_middle(
    layer, parts, grad, normed, factor, lower, upper, masks, gains, weight, slope, x, stat, *rest
):
    if layer == 0:
        given_gain, given_bias, three, grad_in, gain_out, bias_out, out = rest
    else:
        three, grad_in, gain_out, bias_out, out = rest
    total, cross = merged_sums(parts)
    gain_out[0:1] = cross
    bias_out[0:1] = total
    if layer == 0:
        gain_out[1:2] = given_gain[...]
        bias_out[1:2] = given_bias[...]
    total, cross = total * (1.0 / TOTAL), cross * (1.0 / TOTAL)
    scale = gains[layer : layer + 1] * factor[...]

    def conv_grad(grads, rows):
        return scale * (grads - total - rows * cross)

    def side(pair, column):
        values = conv_grad(pair[:, :HALF].astype(F32), pair[:, HALF:].astype(F32))
        mask = masks[:, 2 * layer + column : 2 * layer + column + 1]
        return jnp.where(mask > 0, values, 0.0).astype(BF16)

    three[:, :HALF] = side(upper, 1)
    three[:, HALF : 2 * HALF] = conv_grad(grad[...], normed[...]).astype(BF16)
    three[:, 2 * HALF :] = side(lower, 0)
    values = product_nt(three[...], weight[...]) * slope[...]
    grad_in[...] = values
    normed_in = (x[...].astype(F32) - stat[0:1]) * stat[1:2]
    spread_out(
        out,
        jnp.sum(values, axis=0, keepdims=True),
        jnp.sum(values * normed_in, axis=0, keepdims=True),
    )


def back_entry(layer, parts, grad_in, x, stat, gains, upstream):
    if layer == 0:
        total, cross = parts[:, :CH], parts[:, CH:]
    else:
        total, cross = merged_sums(parts)
    factor = stat[1:2]
    normed = (x[...].astype(F32) - stat[0:1]) * factor
    branch = (gains[layer : layer + 1] * factor) * (
        grad_in[...] - total * (1.0 / TOTAL) - normed * (cross * (1.0 / TOTAL))
    )
    return total, cross, (upstream[...].astype(F32) + branch).astype(BF16)


def k_back_entry(
    parts, grad_in, x, stat, gains, upstream, project, slope, normed, *rest
):
    gain_out, bias_out, stream, grad, pair, out = rest
    bias_out[...], gain_out[...], rows = back_entry(1, parts, grad_in, x, stat, gains, upstream)
    stream[...] = rows
    begin_backward(rows, project, slope[...], normed[...], grad, pair, out)


def k_last(parts, grad_in, x, stat, gains, upstream, given_gain, given_bias, gain_out, bias_out, stream):
    total, cross, stream[...] = back_entry(0, parts, grad_in, x, stat, gains, upstream)
    gain_out[0:1] = cross
    gain_out[1:2] = given_gain[...]
    bias_out[0:1] = total
    bias_out[1:2] = given_bias[...]


def half_of(ref, other):
    half = ref.shape[1] // 2
    place = lax.axis_index("dp")
    place = 1 - place if other else place
    return ref[:, pl.ds(pl.multiple_of(place * half, 128), half)]


def k_give(*refs):
    out, first = refs[-1], 0
    for left, right in zip(refs[0:-1:2], refs[1:-1:2]):
        width = right.shape[1] // 2
        out[:, first : first + width] = product_tn(left[...], half_of(right, True)).astype(BF16)
        first += width


def k_keep(pairs, arrived, *refs):
    out, first = refs[-1], 0
    for i in range(pairs):
        left, right = refs[2 * i], refs[2 * i + 1]
        width = right.shape[1] // 2
        other = arrived[:, first : first + width].astype(F32)
        mine = product_tn(left[...], half_of(right, False))
        out[:, first : first + width] = (mine + other).astype(BF16)
        first += width


def k_gather(parts, other, out):
    for z in range(8):
        rows = slice(8 * z, 8 * z + 8)
        total = parts[0, rows].astype(F32)
        for i in range(1, GROUP):
            total = total + parts[i, rows].astype(F32)
        whole_row = jnp.concatenate([total.astype(BF16), other[rows, :]], axis=1)
        out[z] = whole_row
        out[8 + z] = whole_row


def k_rows(parts, kernel_out, project_out):
    cut, width = 3 * HALF // 2, HALF // 2
    for d in range(2):
        total = parts[8 * d].astype(F32)
        for z in range(1, 8):
            total = total + parts[8 * d + z].astype(F32)
        for layer in range(2):
            first = layer * CH
            kernel_out[layer, :, d * cut : (d + 1) * cut] = total[:, first : first + cut]
            project_out[layer, :, d * width : (d + 1) * width] = total[:, first + cut : first + CH]


def whole(value):
    shape = value.shape
    return pl.BlockSpec(shape, lambda i: (0,) * len(shape))


def in_memory(value):
    return pltpu.with_memory_space_constraint(value, pltpu.HBM)


class Loaded:
    def __init__(self, copy, ref):
        self.copy, self.ref, self.shape = copy, ref, ref.shape
        copy.start()

    def finish(self):
        if self.copy is not None:
            self.copy.wait()
            self.copy = None

    def __getitem__(self, place):
        self.finish()
        return self.ref[place]


class Stored:
    def __init__(self, copy, ref):
        self.copy, self.ref, self.shape, self.started = copy, ref, ref.shape, False

    def start(self):
        if not self.started:
            self.copy.start()
            self.started = True

    def __getitem__(self, place):
        return self.ref[place]

    def __setitem__(self, place, value):
        self.ref[place] = value
        if place is Ellipsis:
            self.start()


def staged(kernel, counts, loaded, stored):
    n_in, n_waits, n_out = counts

    def body(*refs):
        ins, outs = list(refs[:n_in]), list(refs[n_in + n_waits : n_in + n_waits + n_out])
        scratch = list(refs[n_in + n_waits + n_out :])
        sems, late, results = scratch.pop(), [], []
        for place, (i, layer) in enumerate(loaded):
            source = ins[i] if layer is None else ins[i].at[layer]
            buffer = scratch.pop(0)
            ins[i] = Loaded(pltpu.make_async_copy(source, buffer, sems.at[place]), buffer)
            late.append(ins[i])
        for place, i in enumerate(stored, len(loaded)):
            buffer = scratch.pop(0)
            outs[i] = Stored(pltpu.make_async_copy(buffer, outs[i], sems.at[place]), buffer)
            results.append(outs[i])
        kernel(*ins, *outs)
        for value in late:
            value.finish()
        for value in results:
            value.start()
        for value in results:
            value.copy.wait()

    return body


def call(kernel, outs, *operands, name, loaded=(), stored=(), layers=None, waits=(), held=(), flops=1 << 22):
    layers = layers or {}
    in_hbm = pl.BlockSpec(memory_space=pltpu.HBM)
    specs = [in_hbm if i in loaded else whole(value) for i, value in enumerate(operands)]
    specs += [pl.BlockSpec(memory_space=pl.ANY)] * len(waits) + [in_hbm] * len(held)
    shapes = [jax.ShapeDtypeStruct(shape, dtype) for shape, dtype in outs]
    moved = sum(v.size * v.dtype.itemsize for v in list(operands) + shapes)
    scratch = []
    for i in loaded:
        shape = operands[i].shape
        scratch.append(pltpu.VMEM(shape[1:] if i in layers else shape, operands[i].dtype))
    scratch += [pltpu.VMEM(*outs[i]) for i in stored]
    scratch.append(pltpu.SemaphoreType.DMA((max(1, len(loaded) + len(stored)),)))
    body = staged(
        kernel,
        (len(operands), len(waits) + len(held), len(outs)),
        [(i, layers.get(i)) for i in loaded],
        stored,
    )
    return pl.pallas_call(
        body,
        grid=(1,),
        in_specs=specs,
        out_specs=[in_hbm if i in stored else whole(shape) for i, shape in enumerate(shapes)],
        out_shape=[
            pltpu.HBM(shape.shape, shape.dtype) if i in stored else shape
            for i, shape in enumerate(shapes)
        ],
        scratch_shapes=scratch,
        name=name,
        cost_estimate=pl.CostEstimate(flops=flops, bytes_accessed=moved, transcendentals=0),
        compiler_params=pltpu.CompilerParams(vmem_limit_bytes=VMEM_LIMIT),
    )(
        *[in_memory(value) if i in loaded else value for i, value in enumerate(operands)],
        *waits,
        *[in_memory(value) for value in held],
    )


def exchange(value, axes):
    return lax.all_to_all(value, axes, 0, 0, tiled=True)


def over_all(payload, kind, waits=(), held=()):
    first = exchange(payload, FIRST_STAGE)
    (merged,) = call(
        functools.partial(k_merge, kind),
        [(payload.shape, F32)],
        first,
        waits=waits,
        held=held,
        name="merge_" + kind,
    )
    return exchange(merged, SECOND_STAGE), merged


def passed_along(value, steps):
    count = 128
    leading, last = (max(0, -steps), min(count, count - steps))
    return lax.ppermute(value, SEQ, [(source, source + steps) for source in range(leading, last)])


def neighbours(rows, dilation):
    hops = dilation // 64
    return passed_along(rows, hops), passed_along(rows, -hops)


def chip_share(*pairs, waits=(), waits_first=(), held=()):
    operands = [value for pair in pairs for value in pair]
    width = sum(right.shape[1] for _, right in pairs) // 2
    shape = [((CH, width), BF16)]
    flops = 2 * ROWS * CH * width
    count = len(operands)
    (given,) = call(
        k_give,
        shape,
        *operands,
        loaded=tuple(range(count)),
        waits=waits_first,
        name="give",
        flops=flops,
    )
    arrived = swapped(given, "dp", 1)
    (share,) = call(
        functools.partial(k_keep, len(pairs)),
        shape,
        arrived,
        *operands,
        loaded=tuple(range(1, count + 1)),
        stored=(0,),
        waits=waits,
        held=held,
        name="keep",
        flops=flops,
    )
    return share


def swapped(value, axis, step):
    pairs = [(i, i ^ step) for i in range(SIZES[axis])]
    return lax.ppermute(value, axis, pairs)


def rows_over(share, axis):
    return lax.psum_scatter(share, axis, scatter_dimension=0, tiled=True)


def on_device(
    activations,
    segment_ids,
    interval_bounds,
    conv_weight,
    proj_weight,
    gains_in,
    biases_in,
    gains_mid,
    biases_mid,
    cotangent,
):
    windows, local_bins, channels = activations.shape
    position = lax.axis_index(SEQ) * local_bins + jnp.arange(local_bins, dtype=jnp.int32)[None, :]
    labels = jnp.arange(interval_bounds.shape[1] - 1, dtype=jnp.int32)
    matches = segment_ids[:, :, None] == labels[None, None, :]
    starts = jnp.sum(jnp.where(matches, interval_bounds[:, None, :-1], 0), axis=2)
    finishes = jnp.sum(jnp.where(matches, interval_bounds[:, None, 1:], 0), axis=2)
    masks = []
    for dilation in (FIRST_DILATION, SECOND_DILATION):
        masks.append(starts <= position - dilation)
        masks.append(position + dilation < finishes)
    masks = jnp.stack(masks, axis=2).astype(F32).reshape(ROWS, 4)

    wide, narrow = (GROUP, 1, 2 * CH), (GROUP, 1, CH)
    conv_flops = 2 * ROWS * CH * 3 * HALF
    stream_0 = activations.reshape(ROWS, CH)
    grad_2 = cotangent.reshape(ROWS, CH)

    def entry(layer, stream, parts, sides):
        return call(
            functools.partial(k_entry, layer),
            [((ROWS, CH), BF16), ((ROWS, CH), F32), ((ROWS, HALF), F32), ((2, CH), F32), (narrow, F32)],
            parts,
            stream,
            *sides,
            masks,
            conv_weight,
            gains_in,
            biases_in,
            loaded=(5, 6, 7) if layer else (1, 5, 6, 7),
            stored=(0, 1, 3),
            layers={5: layer},
            name="entry",
            flops=conv_flops,
        )

    sides = neighbours(stream_0, FIRST_DILATION)
    (payload,) = call(k_first, [(wide, F32)], stream_0, loaded=(0,), name="first")
    parts, _ = over_all(payload, "moments", sides)
    taps_0, slope_0, conv_0, stat_0, payload = entry(0, stream_0, parts, sides)
    parts, _ = over_all(payload, "moments")
    hidden_0, stream_1, kept_1, slope_mid_0, normed_0, factor_0, payload = call(
        k_middle,
        [
            ((ROWS, HALF), BF16),
            ((ROWS, CH), BF16),
            ((ROWS, CH), BF16),
            ((ROWS, HALF), F32),
            ((ROWS, HALF), F32),
            ((1, HALF), F32),
            (wide, F32),
        ],
        parts,
        conv_0,
        gains_mid,
        biases_mid,
        proj_weight,
        stream_0,
        loaded=(2, 3, 4, 5),
        stored=(0, 2, 3, 4, 5),
        layers={4: 0},
        name="middle",
    )
    sides = neighbours(stream_1, SECOND_DILATION)
    parts, _ = over_all(payload, "moments", sides)
    taps_1, slope_1, conv_1, stat_1, payload = entry(1, stream_1, parts, sides)
    parts, _ = over_all(payload, "moments")
    hidden_1, stream_2, normed_1, factor_1, grad, pair, payload = call(
        k_turn,
        [
            ((ROWS, HALF), BF16),
            ((ROWS, CH), BF16),
            ((ROWS, HALF), F32),
            ((1, HALF), F32),
            ((ROWS, HALF), F32),
            ((ROWS, CH), BF16),
            (narrow, F32),
        ],
        parts,
        conv_1,
        gains_mid,
        biases_mid,
        proj_weight,
        kept_1,
        grad_2,
        loaded=(2, 3, 4, 5, 6),
        stored=(0, 1),
        layers={4: 1},
        name="turn",
    )

    def back_middle(
        layer, parts, grad, normed, factor, sides, slope, stream, stat, *given, held=()
    ):
        rows = 2 - layer
        return call(
            functools.partial(k_back_middle, layer),
            [
                ((ROWS, 3 * HALF), BF16),
                ((ROWS, CH), F32),
                ((rows, HALF), F32),
                ((rows, HALF), F32),
                (wide, F32),
            ],
            parts,
            grad,
            normed,
            factor,
            *sides,
            masks,
            gains_mid,
            conv_weight,
            slope,
            stream,
            stat,
            *given,
            loaded=(7, 8, 9, 10, 11) if layer else (2, 3, 7, 8, 9, 10, 11, 12, 13),
            stored=(0, 2, 3),
            layers={8: layer},
            held=held,
            name="back_middle",
            flops=conv_flops,
        )

    sides = neighbours(pair, SECOND_DILATION)
    parts, _ = over_all(payload, "sums", sides)
    three_1, grad_in, gain_mid, bias_mid, payload = back_middle(
        1, parts, grad, normed_1, factor_1, sides, slope_1, kept_1, stat_1
    )
    parts, merged = over_all(payload, "sums")
    share_1 = chip_share((taps_1, three_1), (grad_2, hidden_1), waits_first=(merged,))
    rows_1 = rows_over(share_1, SECOND_STAGE)
    gain_in, bias_in, grad_1, grad, pair, payload = call(
        k_back_entry,
        [
            ((1, CH), F32),
            ((1, CH), F32),
            ((ROWS, CH), BF16),
            ((ROWS, HALF), F32),
            ((ROWS, CH), BF16),
            (narrow, F32),
        ],
        parts,
        grad_in,
        kept_1,
        stat_1,
        gains_in,
        grad_2,
        proj_weight,
        slope_mid_0,
        normed_0,
        loaded=(2, 3, 4, 5, 6, 7, 8),
        stored=(0, 1, 2),
        layers={6: 0},
        name="back_entry",
    )
    sides = neighbours(pair, FIRST_DILATION)
    parts, _ = over_all(payload, "sums", sides)
    three_0, grad_in, grad_gains_mid, grad_biases_mid, payload = back_middle(
        0,
        parts,
        grad,
        normed_0,
        factor_0,
        sides,
        slope_0,
        stream_0,
        stat_0,
        gain_mid,
        bias_mid,
    )
    (sums,) = call(
        functools.partial(k_merge, "sums"),
        [((1, 2 * CH), F32)],
        exchange(payload, FIRST_STAGE),
        name="merge_sums",
    )
    share_0 = chip_share((taps_0, three_0), (grad_1, hidden_0), waits=(sums,))
    share_0 = exchange(share_0.reshape(GROUP, CH // GROUP, CH), SECOND_STAGE)
    for axis in ("x", "y"):
        for step in (1, 2):
            sums = sums + swapped(sums, axis, step)
    grad_gains_in, grad_biases_in, grad_0 = call(
        k_last,
        [((2, CH), F32), ((2, CH), F32), ((ROWS, CH), BF16)],
        sums,
        grad_in,
        stream_0,
        stat_0,
        gains_in,
        grad_1,
        gain_in,
        bias_in,
        loaded=(2, 3, 4, 5, 6, 7),
        stored=(0, 1, 2),
        name="last",
    )
    (rows,) = call(
        k_gather,
        [((GROUP, 8, 2 * CH), BF16)],
        share_0,
        rows_1,
        loaded=(1,),
        name="gather_rows",
    )
    grad_conv, grad_proj = call(
        k_rows,
        [((2, 8, 3 * HALF), F32), ((2, 8, HALF), F32)],
        exchange(rows, FIRST_STAGE),
        stored=(0, 1),
        name="rows",
    )
    return (
        stream_2.reshape(activations.shape),
        grad_0.reshape(activations.shape),
        grad_conv,
        grad_proj,
        grad_gains_in,
        grad_biases_in,
        grad_gains_mid,
        grad_biases_mid,
    )


def solution(mesh):
    sizes = tuple(SIZES.values())
    split = Mesh(mesh.devices.reshape(sizes), tuple(SIZES))
    bins = P("dp", SEQ, None)
    rows = P(None, SEQ, None)
    in_specs = (bins, P("dp", SEQ), P("dp", None), P(), P(), P(), P(), P(), P(), bins)
    out_specs = (bins, bins, rows, rows, P(), P(), P(), P())
    return jax.shard_map(
        on_device, mesh=split, in_specs=in_specs, out_specs=out_specs, check_vma=False
    )
```

```python
import functools

import jax
import jax.numpy as jnp
from jax import lax
from jax.experimental import pallas as pl
from jax.experimental.pallas import tpu as pltpu
from jax.sharding import Mesh, PartitionSpec as P

FIRST_DILATION = 64
SECOND_DILATION = 512
EPSILON = 1e-05
SIZES = {"dp": 2, "y": 4, "x": 4, "z": 8}
SEQ = ("y", "x", "z")
FIRST_STAGE = ("dp", "z")
SECOND_STAGE = ("y", "x")
GROUP = 16
F32 = jnp.float32
BF16 = jnp.bfloat16
ROWS, CH, HALF = 128, 1024, 512
VMEM_LIMIT = 32 << 20
TOTAL = 32768.0
TANH_SCALE = 0.7978845608028654
CUBE = 0.044715


def gelu(v):
    return 0.5 * v * (1.0 + jnp.tanh(TANH_SCALE * (v + CUBE * (v * v * v))))


def gelu_slope(v):
    square = v * v
    t = jnp.tanh(TANH_SCALE * (v + CUBE * (square * v)))
    half = 0.5 * (1.0 + t)
    slope = half + 0.5 * v * (1.0 - t * t) * (TANH_SCALE * (1.0 + 3.0 * CUBE * square))
    return v * half, slope


def spread_out(out, first, second):
    row = jnp.concatenate([first, second], axis=1)
    for i in range(GROUP):
        out[i] = row


def local_moments(values):
    mean = jnp.sum(values, axis=0, keepdims=True) * (1.0 / ROWS)
    centred = values - mean
    return mean, jnp.sum(centred * centred, axis=0, keepdims=True) * (1.0 / ROWS)


def merged_moments(parts):
    width = parts.shape[2] // 2
    means = [parts[i, :, :width] for i in range(GROUP)]
    mean = sum(means[1:], means[0]) * (1.0 / GROUP)
    square = jnp.zeros_like(mean)
    for i in range(GROUP):
        offset = means[i] - mean
        square = square + (parts[i, :, width:] + offset * offset)
    return mean, square * (1.0 / GROUP)


def merged_sums(parts):
    width = parts.shape[2] // 2
    total = parts[0]
    for i in range(1, GROUP):
        total = total + parts[i]
    return total[:, :width], total[:, width:]


def product(left, right):
    return jnp.dot(left, right, preferred_element_type=F32)


def product_nt(left, right):
    return lax.dot_general(left, right, (((1,), (1,)), ((), ())), preferred_element_type=F32)


def product_tn(left, right):
    return lax.dot_general(left, right, (((0,), (0,)), ((), ())), preferred_element_type=F32)


def k_first(x, out):
    spread_out(out, *local_moments(x[...].astype(F32)))


def k_merge(kind, parts, *rest):
    out = rest[-1]
    merge = merged_moments if kind == "moments" else merged_sums
    if out.shape[0] == 1:
        out[...] = jnp.concatenate(merge(parts), axis=1)
    else:
        spread_out(out, *merge(parts))


def k_entry(layer, parts, x, lower, upper, masks, weight, gains, biases, taps, slope, conv, stat, out):
    mean, spread = merged_moments(parts)
    factor = lax.rsqrt(spread + EPSILON)
    gain, bias = gains[layer : layer + 1], biases[layer : layer + 1]
    active, slope_in = gelu_slope((x[...].astype(F32) - mean) * factor * gain + bias)
    slope[...] = slope_in
    centre = active.astype(BF16)
    taps[...] = centre
    stat[...] = jnp.concatenate([mean, factor], axis=0)

    def side(rows, column):
        values = gelu((rows[...].astype(F32) - mean) * factor * gain + bias)
        mask = masks[:, 2 * layer + column : 2 * layer + column + 1]
        return jnp.where(mask > 0, values, 0.0).astype(BF16)

    result = product(centre, weight[:, HALF : 2 * HALF])
    result = result + product(side(lower, 0), weight[:, :HALF])
    result = result + product(side(upper, 1), weight[:, 2 * HALF :])
    conv[...] = result
    spread_out(out, *local_moments(result))


def middle(layer, parts, conv, gains, biases, project, x):
    mean, spread = merged_moments(parts)
    factor = lax.rsqrt(spread + EPSILON)
    normed = (conv[...] - mean) * factor
    active, slope = gelu_slope(normed * gains[layer : layer + 1] + biases[layer : layer + 1])
    hidden = active.astype(BF16)
    following = (x[...].astype(F32) + product_nt(hidden, project[...])).astype(BF16)
    return factor, normed, slope, hidden, following


def k_middle(
    parts, conv, gains, biases, project, x, hidden, following, kept, slope, normed, factor, out
):
    factor[...], normed[...], slope[...], hidden[...], rows = middle(
        0, parts, conv, gains, biases, project, x
    )
    following[...] = rows
    kept[...] = rows
    spread_out(out, *local_moments(rows.astype(F32)))


def begin_backward(upstream, project, slope, normed, grad, pair, out):
    values = product(upstream, project[...]) * slope
    grad[...] = values
    pair[:, :HALF] = values.astype(BF16)
    pair[:, HALF:] = normed.astype(BF16)
    spread_out(
        out,
        jnp.sum(values, axis=0, keepdims=True),
        jnp.sum(values * normed, axis=0, keepdims=True),
    )


def k_turn(parts, conv, gains, biases, project, x, upstream, hidden, following, normed, factor, grad, pair, out):
    factor[...], rows, slope, hidden[...], following[...] = middle(
        1, parts, conv, gains, biases, project, x
    )
    normed[...] = rows
    begin_backward(upstream[...], project, slope, rows, grad, pair, out)


def k_back_middle(
    layer, parts, grad, normed, factor, lower, upper, masks, gains, weight, slope, x, stat, *rest
):
    if layer == 0:
        given_gain, given_bias, three, grad_in, gain_out, bias_out, out = rest
    else:
        three, grad_in, gain_out, bias_out, out = rest
    total, cross = merged_sums(parts)
    gain_out[0:1] = cross
    bias_out[0:1] = total
    if layer == 0:
        gain_out[1:2] = given_gain[...]
        bias_out[1:2] = given_bias[...]
    total, cross = total * (1.0 / TOTAL), cross * (1.0 / TOTAL)
    scale = gains[layer : layer + 1] * factor[...]

    def conv_grad(grads, rows):
        return scale * (grads - total - rows * cross)

    def side(pair, column):
        values = conv_grad(pair[:, :HALF].astype(F32), pair[:, HALF:].astype(F32))
        mask = masks[:, 2 * layer + column : 2 * layer + column + 1]
        return jnp.where(mask > 0, values, 0.0).astype(BF16)

    three[:, :HALF] = side(upper, 1)
    three[:, HALF : 2 * HALF] = conv_grad(grad[...], normed[...]).astype(BF16)
    three[:, 2 * HALF :] = side(lower, 0)
    values = product_nt(three[...], weight[...]) * slope[...]
    grad_in[...] = values
    normed_in = (x[...].astype(F32) - stat[0:1]) * stat[1:2]
    spread_out(
        out,
        jnp.sum(values, axis=0, keepdims=True),
        jnp.sum(values * normed_in, axis=0, keepdims=True),
    )


def back_entry(layer, parts, grad_in, x, stat, gains, upstream):
    if layer == 0:
        total, cross = parts[:, :CH], parts[:, CH:]
    else:
        total, cross = merged_sums(parts)
    factor = stat[1:2]
    normed = (x[...].astype(F32) - stat[0:1]) * factor
    branch = (gains[layer : layer + 1] * factor) * (
        grad_in[...] - total * (1.0 / TOTAL) - normed * (cross * (1.0 / TOTAL))
    )
    return total, cross, (upstream[...].astype(F32) + branch).astype(BF16)


def k_back_entry(
    parts, grad_in, x, stat, gains, upstream, project, slope, normed, *rest
):
    gain_out, bias_out, stream, grad, pair, out = rest
    bias_out[...], gain_out[...], rows = back_entry(1, parts, grad_in, x, stat, gains, upstream)
    stream[...] = rows
    begin_backward(rows, project, slope[...], normed[...], grad, pair, out)


def k_last(parts, grad_in, x, stat, gains, upstream, given_gain, given_bias, gain_out, bias_out, stream):
    total, cross, stream[...] = back_entry(0, parts, grad_in, x, stat, gains, upstream)
    gain_out[0:1] = cross
    gain_out[1:2] = given_gain[...]
    bias_out[0:1] = total
    bias_out[1:2] = given_bias[...]


def half_of(ref, other):
    half = ref.shape[1] // 2
    place = lax.axis_index("dp")
    place = 1 - place if other else place
    return ref[:, pl.ds(pl.multiple_of(place * half, 128), half)]


def k_give(*refs):
    out, first = refs[-1], 0
    for left, right in zip(refs[0:-1:2], refs[1:-1:2]):
        width = right.shape[1] // 2
        out[:, first : first + width] = product_tn(left[...], half_of(right, True)).astype(BF16)
        first += width


def k_keep(pairs, arrived, *refs):
    out, first = refs[-1], 0
    for i in range(pairs):
        left, right = refs[2 * i], refs[2 * i + 1]
        width = right.shape[1] // 2
        other = arrived[:, first : first + width].astype(F32)
        mine = product_tn(left[...], half_of(right, False))
        out[:, first : first + width] = (mine + other).astype(BF16)
        first += width


def k_gather(parts, other, out):
    for z in range(8):
        rows = slice(8 * z, 8 * z + 8)
        total = parts[0, rows].astype(F32)
        for i in range(1, GROUP):
            total = total + parts[i, rows].astype(F32)
        whole_row = jnp.concatenate([total.astype(BF16), other[rows, :]], axis=1)
        out[z] = whole_row
        out[8 + z] = whole_row


def k_rows(parts, kernel_out, project_out):
    cut, width = 3 * HALF // 2, HALF // 2
    for d in range(2):
        total = parts[8 * d].astype(F32)
        for z in range(1, 8):
            total = total + parts[8 * d + z].astype(F32)
        for layer in range(2):
            first = layer * CH
            kernel_out[layer, :, d * cut : (d + 1) * cut] = total[:, first : first + cut]
            project_out[layer, :, d * width : (d + 1) * width] = total[:, first + cut : first + CH]


def k_pass(value, out):
    out[...] = value[...]


def whole(value):
    shape = value.shape
    return pl.BlockSpec(shape, lambda i: (0,) * len(shape))


def in_memory(value):
    return pltpu.with_memory_space_constraint(value, pltpu.HBM)


class Loaded:
    def __init__(self, copy, ref):
        self.copy, self.ref, self.shape = copy, ref, ref.shape
        copy.start()

    def finish(self):
        if self.copy is not None:
            self.copy.wait()
            self.copy = None

    def __getitem__(self, place):
        self.finish()
        return self.ref[place]


class Stored:
    def __init__(self, copy, ref):
        self.copy, self.ref, self.shape, self.started = copy, ref, ref.shape, False

    def start(self):
        if not self.started:
            self.copy.start()
            self.started = True

    def __getitem__(self, place):
        return self.ref[place]

    def __setitem__(self, place, value):
        self.ref[place] = value
        if place is Ellipsis:
            self.start()


def staged(kernel, counts, loaded, stored):
    n_in, n_waits, n_out = counts

    def body(*refs):
        ins, outs = list(refs[:n_in]), list(refs[n_in + n_waits : n_in + n_waits + n_out])
        scratch = list(refs[n_in + n_waits + n_out :])
        sems, late, results = scratch.pop(), [], []
        for place, (i, layer) in enumerate(loaded):
            source = ins[i] if layer is None else ins[i].at[layer]
            buffer = scratch.pop(0)
            ins[i] = Loaded(pltpu.make_async_copy(source, buffer, sems.at[place]), buffer)
            late.append(ins[i])
        for place, i in enumerate(stored, len(loaded)):
            buffer = scratch.pop(0)
            outs[i] = Stored(pltpu.make_async_copy(buffer, outs[i], sems.at[place]), buffer)
            results.append(outs[i])
        kernel(*ins, *outs)
        for value in late:
            value.finish()
        for value in results:
            value.start()
        for value in results:
            value.copy.wait()

    return body


def call(kernel, outs, *operands, name, loaded=(), free=(), stored=(), layers=None, waits=(), held=(), flops=1 << 22):
    layers = layers or {}
    in_hbm = pl.BlockSpec(memory_space=pltpu.HBM)
    specs = [
        pl.BlockSpec(memory_space=pl.ANY) if i in free else in_hbm if i in loaded else whole(value)
        for i, value in enumerate(operands)
    ]
    specs += [pl.BlockSpec(memory_space=pl.ANY)] * len(waits) + [in_hbm] * len(held)
    shapes = [jax.ShapeDtypeStruct(shape, dtype) for shape, dtype in outs]
    moved = sum(v.size * v.dtype.itemsize for v in list(operands) + shapes)
    scratch = []
    for i in loaded:
        shape = operands[i].shape
        scratch.append(pltpu.VMEM(shape[1:] if i in layers else shape, operands[i].dtype))
    scratch += [pltpu.VMEM(*outs[i]) for i in stored]
    scratch.append(pltpu.SemaphoreType.DMA((max(1, len(loaded) + len(stored)),)))
    body = staged(
        kernel,
        (len(operands), len(waits) + len(held), len(outs)),
        [(i, layers.get(i)) for i in loaded],
        stored,
    )
    return pl.pallas_call(
        body,
        grid=(1,),
        in_specs=specs,
        out_specs=[in_hbm if i in stored else whole(shape) for i, shape in enumerate(shapes)],
        out_shape=[
            pltpu.HBM(shape.shape, shape.dtype) if i in stored else shape
            for i, shape in enumerate(shapes)
        ],
        scratch_shapes=scratch,
        name=name,
        cost_estimate=pl.CostEstimate(flops=flops, bytes_accessed=moved, transcendentals=0),
        compiler_params=pltpu.CompilerParams(vmem_limit_bytes=VMEM_LIMIT),
    )(
        *[in_memory(v) if i in loaded and i not in free else v for i, v in enumerate(operands)],
        *waits,
        *[in_memory(value) for value in held],
    )


def exchange(value, axes):
    return lax.all_to_all(value, axes, 0, 0, tiled=True)


def over_all(payload, kind, waits=(), held=()):
    first = exchange(payload, FIRST_STAGE)
    (merged,) = call(
        functools.partial(k_merge, kind),
        [(payload.shape, F32)],
        first,
        waits=waits,
        held=held,
        name="merge_" + kind,
    )
    return exchange(merged, SECOND_STAGE), merged


def passed_along(value, steps):
    count = 128
    leading, last = (max(0, -steps), min(count, count - steps))
    return lax.ppermute(value, SEQ, [(source, source + steps) for source in range(leading, last)])


def neighbours(rows, dilation):
    hops = dilation // 64
    return passed_along(rows, hops), passed_along(rows, -hops)


def chip_share(*pairs, waits=(), waits_first=(), held=()):
    operands = [value for pair in pairs for value in pair]
    width = sum(right.shape[1] for _, right in pairs) // 2
    shape = [((CH, width), BF16)]
    flops = 2 * ROWS * CH * width
    count = len(operands)
    (given,) = call(
        k_give,
        shape,
        *operands,
        loaded=tuple(range(count)),
        waits=waits_first,
        name="give",
        flops=flops,
    )
    arrived = swapped(given, "dp", 1)
    (share,) = call(
        functools.partial(k_keep, len(pairs)),
        shape,
        arrived,
        *operands,
        loaded=tuple(range(1, count + 1)),
        stored=(0,),
        waits=waits,
        held=held,
        name="keep",
        flops=flops,
    )
    return share


def swapped(value, axis, step):
    pairs = [(i, i ^ step) for i in range(SIZES[axis])]
    return lax.ppermute(value, axis, pairs)


def rows_over(share, axis):
    return lax.psum_scatter(share, axis, scatter_dimension=0, tiled=True)


def on_device(
    activations,
    segment_ids,
    interval_bounds,
    conv_weight,
    proj_weight,
    gains_in,
    biases_in,
    gains_mid,
    biases_mid,
    cotangent,
):
    windows, local_bins, channels = activations.shape
    position = lax.axis_index(SEQ) * local_bins + jnp.arange(local_bins, dtype=jnp.int32)[None, :]
    labels = jnp.arange(interval_bounds.shape[1] - 1, dtype=jnp.int32)
    matches = segment_ids[:, :, None] == labels[None, None, :]
    starts = jnp.sum(jnp.where(matches, interval_bounds[:, None, :-1], 0), axis=2)
    finishes = jnp.sum(jnp.where(matches, interval_bounds[:, None, 1:], 0), axis=2)
    masks = []
    for dilation in (FIRST_DILATION, SECOND_DILATION):
        masks.append(starts <= position - dilation)
        masks.append(position + dilation < finishes)
    masks = jnp.stack(masks, axis=2).astype(F32).reshape(ROWS, 4)

    wide, narrow = (GROUP, 1, 2 * CH), (GROUP, 1, CH)
    conv_flops = 2 * ROWS * CH * 3 * HALF
    stream_0 = activations.reshape(ROWS, CH)
    grad_2 = cotangent.reshape(ROWS, CH)

    def entry(layer, stream, parts, sides):
        return call(
            functools.partial(k_entry, layer),
            [((ROWS, CH), BF16), ((ROWS, CH), F32), ((ROWS, HALF), F32), ((2, CH), F32), (narrow, F32)],
            parts,
            stream,
            *sides,
            masks,
            conv_weight,
            gains_in,
            biases_in,
            loaded=(5, 6, 7) if layer else (1, 5, 6, 7),
            free=(6, 7) if layer else (),
            stored=(0, 1, 3),
            layers={5: layer},
            name="entry",
            flops=conv_flops,
        )

    sides = neighbours(stream_0, FIRST_DILATION)
    (payload,) = call(k_first, [(wide, F32)], stream_0, loaded=(0,), name="first")
    parts, _ = over_all(payload, "moments", sides)
    taps_0, slope_0, conv_0, stat_0, payload = entry(0, stream_0, parts, sides)
    parts, _ = over_all(payload, "moments")
    hidden_0, stream_1, kept_1, slope_mid_0, normed_0, factor_0, payload = call(
        k_middle,
        [
            ((ROWS, HALF), BF16),
            ((ROWS, CH), BF16),
            ((ROWS, CH), BF16),
            ((ROWS, HALF), F32),
            ((ROWS, HALF), F32),
            ((1, HALF), F32),
            (wide, F32),
        ],
        parts,
        conv_0,
        gains_mid,
        biases_mid,
        proj_weight,
        stream_0,
        loaded=(2, 3, 4, 5),
        free=(2, 3, 4, 5),
        stored=(0, 2, 3, 4, 5),
        layers={4: 0},
        name="middle",
    )
    sides = neighbours(stream_1, SECOND_DILATION)
    parts, _ = over_all(payload, "moments", sides)
    taps_1, slope_1, conv_1, stat_1, payload = entry(1, stream_1, parts, sides)
    parts, _ = over_all(payload, "moments")
    hidden_1, stream_2, normed_1, factor_1, grad, pair, payload = call(
        k_turn,
        [
            ((ROWS, HALF), BF16),
            ((ROWS, CH), BF16),
            ((ROWS, HALF), F32),
            ((1, HALF), F32),
            ((ROWS, HALF), F32),
            ((ROWS, CH), BF16),
            (narrow, F32),
        ],
        parts,
        conv_1,
        gains_mid,
        biases_mid,
        proj_weight,
        kept_1,
        grad_2,
        loaded=(2, 3, 4, 5, 6),
        free=(2, 3, 4, 5, 6),
        stored=(0, 1),
        layers={4: 1},
        name="turn",
    )

    def back_middle(
        layer, parts, grad, normed, factor, sides, slope, stream, stat, *given, held=()
    ):
        rows = 2 - layer
        return call(
            functools.partial(k_back_middle, layer),
            [
                ((ROWS, 3 * HALF), BF16),
                ((ROWS, CH), F32),
                ((rows, HALF), F32),
                ((rows, HALF), F32),
                (wide, F32),
            ],
            parts,
            grad,
            normed,
            factor,
            *sides,
            masks,
            gains_mid,
            conv_weight,
            slope,
            stream,
            stat,
            *given,
            loaded=(7, 8, 9, 10, 11) if layer else (2, 3, 7, 8, 9, 10, 11, 12, 13),
            free=(7, 9, 10, 11) if layer else (2, 3, 7, 9, 10, 11, 12, 13),
            stored=(0, 2, 3),
            layers={8: layer},
            held=held,
            name="back_middle",
            flops=conv_flops,
        )

    sides = neighbours(pair, SECOND_DILATION)
    parts, _ = over_all(payload, "sums", sides)
    three_1, grad_in, gain_mid, bias_mid, payload = back_middle(
        1, parts, grad, normed_1, factor_1, sides, slope_1, kept_1, stat_1
    )
    parts, merged_1 = over_all(payload, "sums")
    gain_in, bias_in, grad_1, grad, pair, payload = call(
        k_back_entry,
        [
            ((1, CH), F32),
            ((1, CH), F32),
            ((ROWS, CH), BF16),
            ((ROWS, HALF), F32),
            ((ROWS, CH), BF16),
            (narrow, F32),
        ],
        parts,
        grad_in,
        kept_1,
        stat_1,
        gains_in,
        grad_2,
        proj_weight,
        slope_mid_0,
        normed_0,
        loaded=(2, 3, 4, 5, 6, 7, 8),
        free=(2, 3, 4, 5, 6, 7, 8),
        stored=(0, 1, 2),
        layers={6: 0},
        name="back_entry",
    )
    sides = neighbours(pair, FIRST_DILATION)
    parts, merged_0 = over_all(payload, "sums", sides)
    share_1 = chip_share(
        (taps_1, three_1), (grad_2, hidden_1), waits_first=(merged_1,), waits=(merged_0,)
    )
    rows_1 = rows_over(share_1, "y")
    three_0, grad_in, grad_gains_mid, grad_biases_mid, payload = back_middle(
        0,
        parts,
        grad,
        normed_0,
        factor_0,
        sides,
        slope_0,
        stream_0,
        stat_0,
        gain_mid,
        bias_mid,
    )
    (sums,) = call(
        functools.partial(k_merge, "sums"),
        [((1, 2 * CH), F32)],
        exchange(payload, FIRST_STAGE),
        name="merge_sums",
    )
    share_0 = chip_share((taps_0, three_0), (grad_1, hidden_0), waits=(sums,))
    (rows_1,) = call(
        k_pass,
        [(rows_1.shape, BF16)],
        rows_1,
        loaded=(0,),
        stored=(0,),
        held=(share_0,),
        name="pass",
    )
    rows_1 = rows_over(rows_1, "x")
    share_0 = exchange(share_0.reshape(GROUP, CH // GROUP, CH), SECOND_STAGE)
    for axis in ("x", "y"):
        for step in (1, 2):
            sums = sums + swapped(sums, axis, step)
    grad_gains_in, grad_biases_in, grad_0 = call(
        k_last,
        [((2, CH), F32), ((2, CH), F32), ((ROWS, CH), BF16)],
        sums,
        grad_in,
        stream_0,
        stat_0,
        gains_in,
        grad_1,
        gain_in,
        bias_in,
        loaded=(2, 3, 4, 5, 6, 7),
        free=(2, 3, 4, 5, 6, 7),
        stored=(0, 1, 2),
        name="last",
    )
    (rows,) = call(
        k_gather,
        [((GROUP, 8, 2 * CH), BF16)],
        share_0,
        rows_1,
        loaded=(1,),
        name="gather_rows",
    )
    grad_conv, grad_proj = call(
        k_rows,
        [((2, 8, 3 * HALF), F32), ((2, 8, HALF), F32)],
        exchange(rows, FIRST_STAGE),
        stored=(0, 1),
        name="rows",
    )
    return (
        stream_2.reshape(activations.shape),
        grad_0.reshape(activations.shape),
        grad_conv,
        grad_proj,
        grad_gains_in,
        grad_biases_in,
        grad_gains_mid,
        grad_biases_mid,
    )


def solution(mesh):
    sizes = tuple(SIZES.values())
    split = Mesh(mesh.devices.reshape(sizes), tuple(SIZES))
    bins = P("dp", SEQ, None)
    rows = P(None, SEQ, None)
    in_specs = (bins, P("dp", SEQ), P("dp", None), P(), P(), P(), P(), P(), P(), bins)
    out_specs = (bins, bins, rows, rows, P(), P(), P(), P())
    return jax.shard_map(
        on_device, mesh=split, in_specs=in_specs, out_specs=out_specs, check_vma=False
    )
```

```python
import functools

import jax
import jax.numpy as jnp
from jax import lax
from jax.experimental import pallas as pl
from jax.experimental.pallas import tpu as pltpu
from jax.sharding import Mesh, PartitionSpec as P

FIRST_DILATION = 64
SECOND_DILATION = 512
EPSILON = 1e-05
SIZES = {"dp": 2, "y": 4, "x": 4, "z": 8}
SEQ = ("y", "x", "z")
FIRST_STAGE = ("dp", "z")
SECOND_STAGE = ("y", "x")
GROUP = 16
F32 = jnp.float32
BF16 = jnp.bfloat16
ROWS, CH, HALF = 128, 1024, 512
VMEM_LIMIT = 32 << 20
TOTAL = 32768.0
TANH_SCALE = 0.7978845608028654
CUBE = 0.044715


def gelu(v):
    return 0.5 * v * (1.0 + jnp.tanh(TANH_SCALE * (v + CUBE * (v * v * v))))


def gelu_slope(v):
    square = v * v
    t = jnp.tanh(TANH_SCALE * (v + CUBE * (square * v)))
    half = 0.5 * (1.0 + t)
    slope = half + 0.5 * v * (1.0 - t * t) * (TANH_SCALE * (1.0 + 3.0 * CUBE * square))
    return v * half, slope


def spread_out(out, first, second):
    row = jnp.concatenate([first, second], axis=1)
    for i in range(out.shape[0]):
        out[i] = row


def local_moments(values):
    mean = jnp.sum(values, axis=0, keepdims=True) * (1.0 / ROWS)
    centred = values - mean
    return mean, jnp.sum(centred * centred, axis=0, keepdims=True) * (1.0 / ROWS)


def merged_moments(parts):
    width = parts.shape[2] // 2
    means = [parts[i, :, :width] for i in range(GROUP)]
    mean = sum(means[1:], means[0]) * (1.0 / GROUP)
    square = jnp.zeros_like(mean)
    for i in range(GROUP):
        offset = means[i] - mean
        square = square + (parts[i, :, width:] + offset * offset)
    return mean, square * (1.0 / GROUP)


def merged_sums(parts):
    width = parts.shape[2] // 2
    total = parts[0]
    for i in range(1, GROUP):
        total = total + parts[i]
    return total[:, :width], total[:, width:]


def product(left, right):
    return jnp.dot(left, right, preferred_element_type=F32)


def product_nt(left, right):
    return lax.dot_general(left, right, (((1,), (1,)), ((), ())), preferred_element_type=F32)


def product_tn(left, right):
    return lax.dot_general(left, right, (((0,), (0,)), ((), ())), preferred_element_type=F32)


def k_first(x, out):
    spread_out(out, *local_moments(x[...].astype(F32)))


def k_merge(kind, parts, out):
    merge = merged_moments if kind == "moments" else merged_sums
    spread_out(out, *merge(parts))


def k_entry(layer, parts, x, lower, upper, masks, weight, gains, biases, taps, slope, conv, stat, out):
    mean, spread = merged_moments(parts)
    factor = lax.rsqrt(spread + EPSILON)
    gain, bias = gains[layer : layer + 1], biases[layer : layer + 1]
    active, slope_in = gelu_slope((x[...].astype(F32) - mean) * factor * gain + bias)
    slope[...] = slope_in
    centre = active.astype(BF16)
    taps[...] = centre
    stat[...] = jnp.concatenate([mean, factor], axis=0)

    def side(rows, column):
        values = gelu((rows[...].astype(F32) - mean) * factor * gain + bias)
        mask = masks[:, 2 * layer + column : 2 * layer + column + 1]
        return jnp.where(mask > 0, values, 0.0).astype(BF16)

    result = product(centre, weight[:, HALF : 2 * HALF])
    result = result + product(side(lower, 0), weight[:, :HALF])
    result = result + product(side(upper, 1), weight[:, 2 * HALF :])
    conv[...] = result
    spread_out(out, *local_moments(result))


def middle(layer, parts, conv, gains, biases, project, x):
    mean, spread = merged_moments(parts)
    factor = lax.rsqrt(spread + EPSILON)
    normed = (conv[...] - mean) * factor
    active, slope = gelu_slope(normed * gains[layer : layer + 1] + biases[layer : layer + 1])
    hidden = active.astype(BF16)
    following = (x[...].astype(F32) + product_nt(hidden, project[...])).astype(BF16)
    return factor, normed, slope, hidden, following


def k_middle(
    parts, conv, gains, biases, project, x, hidden, following, kept, slope, normed, factor, out
):
    factor[...], normed[...], slope[...], hidden[...], rows = middle(
        0, parts, conv, gains, biases, project, x
    )
    following[...] = rows
    kept[...] = rows
    spread_out(out, *local_moments(rows.astype(F32)))


def begin_backward(upstream, project, slope, normed, grad, pair, out):
    values = product(upstream, project[...]) * slope
    grad[...] = values
    pair[:, :HALF] = values.astype(BF16)
    pair[:, HALF:] = normed.astype(BF16)
    spread_out(
        out,
        jnp.sum(values, axis=0, keepdims=True),
        jnp.sum(values * normed, axis=0, keepdims=True),
    )


def k_turn(parts, conv, gains, biases, project, x, upstream, hidden, following, normed, factor, grad, pair, out):
    factor[...], rows, slope, hidden[...], following[...] = middle(
        1, parts, conv, gains, biases, project, x
    )
    normed[...] = rows
    begin_backward(upstream[...], project, slope, rows, grad, pair, out)


def k_back_middle(
    layer, parts, grad, normed, factor, lower, upper, masks, gains, weight, slope, x, stat, *rest
):
    if layer == 0:
        given_gain, given_bias, three, grad_in, gain_out, bias_out, out = rest
    else:
        three, grad_in, gain_out, bias_out, out = rest
    total, cross = merged_sums(parts)
    gain_out[0:1] = cross
    bias_out[0:1] = total
    if layer == 0:
        gain_out[1:2] = given_gain[...]
        bias_out[1:2] = given_bias[...]
    total, cross = total * (1.0 / TOTAL), cross * (1.0 / TOTAL)
    scale = gains[layer : layer + 1] * factor[...]

    def conv_grad(grads, rows):
        return scale * (grads - total - rows * cross)

    def side(pair, column):
        values = conv_grad(pair[:, :HALF].astype(F32), pair[:, HALF:].astype(F32))
        mask = masks[:, 2 * layer + column : 2 * layer + column + 1]
        return jnp.where(mask > 0, values, 0.0).astype(BF16)

    three[:, :HALF] = side(upper, 1)
    three[:, HALF : 2 * HALF] = conv_grad(grad[...], normed[...]).astype(BF16)
    three[:, 2 * HALF :] = side(lower, 0)
    values = product_nt(three[...], weight[...]) * slope[...]
    grad_in[...] = values
    normed_in = (x[...].astype(F32) - stat[0:1]) * stat[1:2]
    spread_out(
        out,
        jnp.sum(values, axis=0, keepdims=True),
        jnp.sum(values * normed_in, axis=0, keepdims=True),
    )


def back_entry(layer, parts, grad_in, x, stat, gains, upstream):
    if layer == 0:
        total, cross = parts[0, :, :CH], parts[0, :, CH:]
    else:
        total, cross = merged_sums(parts)
    factor = stat[1:2]
    normed = (x[...].astype(F32) - stat[0:1]) * factor
    branch = (gains[layer : layer + 1] * factor) * (
        grad_in[...] - total * (1.0 / TOTAL) - normed * (cross * (1.0 / TOTAL))
    )
    return total, cross, (upstream[...].astype(F32) + branch).astype(BF16)


def k_back_entry(
    parts, grad_in, x, stat, gains, upstream, project, slope, normed, *rest
):
    gain_out, bias_out, stream, grad, pair, out = rest
    bias_out[...], gain_out[...], rows = back_entry(1, parts, grad_in, x, stat, gains, upstream)
    stream[...] = rows
    begin_backward(rows, project, slope[...], normed[...], grad, pair, out)


def k_last(parts, grad_in, x, stat, gains, upstream, given_gain, given_bias, gain_out, bias_out, stream):
    total, cross, stream[...] = back_entry(0, parts, grad_in, x, stat, gains, upstream)
    gain_out[0:1] = cross
    gain_out[1:2] = given_gain[...]
    bias_out[0:1] = total
    bias_out[1:2] = given_bias[...]


def half_of(ref, other):
    half = ref.shape[1] // 2
    place = lax.axis_index("dp")
    place = 1 - place if other else place
    return ref[:, pl.ds(pl.multiple_of(place * half, 128), half)]


def k_give(*refs):
    out, first = refs[-1], 0
    for left, right in zip(refs[0:-1:2], refs[1:-1:2]):
        width = right.shape[1] // 2
        out[:, first : first + width] = product_tn(left[...], half_of(right, True)).astype(BF16)
        first += width


def k_keep(pairs, arrived, *refs):
    out, first = refs[-1], 0
    for i in range(pairs):
        left, right = refs[2 * i], refs[2 * i + 1]
        width = right.shape[1] // 2
        other = arrived[:, first : first + width].astype(F32)
        mine = product_tn(left[...], half_of(right, False))
        out[:, first : first + width] = (mine + other).astype(BF16)
        first += width


def k_gather(parts, other, out):
    for z in range(8):
        rows = slice(8 * z, 8 * z + 8)
        total = parts[0, rows].astype(F32)
        for i in range(1, GROUP):
            total = total + parts[i, rows].astype(F32)
        whole_row = jnp.concatenate([total.astype(BF16), other[rows, :]], axis=1)
        out[z] = whole_row
        out[8 + z] = whole_row


def k_rows(parts, kernel_out, project_out):
    cut, width = 3 * HALF // 2, HALF // 2
    for d in range(2):
        total = parts[8 * d].astype(F32)
        for z in range(1, 8):
            total = total + parts[8 * d + z].astype(F32)
        for layer in range(2):
            first = layer * CH
            kernel_out[layer, :, d * cut : (d + 1) * cut] = total[:, first : first + cut]
            project_out[layer, :, d * width : (d + 1) * width] = total[:, first + cut : first + CH]


def k_merge_first(parts, x, out, sent):
    sent[...] = x[...]
    spread_out(out, *merged_moments(parts))


def k_pass(value, out):
    out[...] = value[...]


def whole(value):
    shape = value.shape
    return pl.BlockSpec(shape, lambda i: (0,) * len(shape))


def in_memory(value):
    return pltpu.with_memory_space_constraint(value, pltpu.HBM)


class Loaded:
    def __init__(self, copy, ref):
        self.copy, self.ref, self.shape = copy, ref, ref.shape
        copy.start()

    def finish(self):
        if self.copy is not None:
            self.copy.wait()
            self.copy = None

    def __getitem__(self, place):
        self.finish()
        return self.ref[place]


class Stored:
    def __init__(self, copy, ref):
        self.copy, self.ref, self.shape, self.started = copy, ref, ref.shape, False

    def start(self):
        if not self.started:
            self.copy.start()
            self.started = True

    def __getitem__(self, place):
        return self.ref[place]

    def __setitem__(self, place, value):
        self.ref[place] = value
        if place is Ellipsis:
            self.start()


def staged(kernel, counts, loaded, stored):
    n_in, n_waits, n_out = counts

    def body(*refs):
        ins, outs = list(refs[:n_in]), list(refs[n_in + n_waits : n_in + n_waits + n_out])
        scratch = list(refs[n_in + n_waits + n_out :])
        sems, late, results = scratch.pop(), [], []
        for place, (i, layer) in enumerate(loaded):
            source = ins[i] if layer is None else ins[i].at[layer]
            buffer = scratch.pop(0)
            ins[i] = Loaded(pltpu.make_async_copy(source, buffer, sems.at[place]), buffer)
            late.append(ins[i])
        for place, i in enumerate(stored, len(loaded)):
            buffer = scratch.pop(0)
            outs[i] = Stored(pltpu.make_async_copy(buffer, outs[i], sems.at[place]), buffer)
            results.append(outs[i])
        kernel(*ins, *outs)
        for value in late:
            value.finish()
        for value in results:
            value.start()
        for value in results:
            value.copy.wait()

    return body


def call(kernel, outs, *operands, name, loaded=(), free=(), stored=(), layers=None, waits=(), held=(), flops=1 << 22):
    layers = layers or {}
    in_hbm = pl.BlockSpec(memory_space=pltpu.HBM)
    specs = [
        pl.BlockSpec(memory_space=pl.ANY) if i in free else in_hbm if i in loaded else whole(value)
        for i, value in enumerate(operands)
    ]
    specs += [pl.BlockSpec(memory_space=pl.ANY)] * len(waits) + [in_hbm] * len(held)
    shapes = [jax.ShapeDtypeStruct(shape, dtype) for shape, dtype in outs]
    moved = sum(v.size * v.dtype.itemsize for v in list(operands) + shapes)
    scratch = []
    for i in loaded:
        shape = operands[i].shape
        scratch.append(pltpu.VMEM(shape[1:] if i in layers else shape, operands[i].dtype))
    scratch += [pltpu.VMEM(*outs[i]) for i in stored]
    scratch.append(pltpu.SemaphoreType.DMA((max(1, len(loaded) + len(stored)),)))
    body = staged(
        kernel,
        (len(operands), len(waits) + len(held), len(outs)),
        [(i, layers.get(i)) for i in loaded],
        stored,
    )
    return pl.pallas_call(
        body,
        grid=(1,),
        in_specs=specs,
        out_specs=[in_hbm if i in stored else whole(shape) for i, shape in enumerate(shapes)],
        out_shape=[
            pltpu.HBM(shape.shape, shape.dtype) if i in stored else shape
            for i, shape in enumerate(shapes)
        ],
        scratch_shapes=scratch,
        name=name,
        cost_estimate=pl.CostEstimate(flops=flops, bytes_accessed=moved, transcendentals=0),
        compiler_params=pltpu.CompilerParams(vmem_limit_bytes=VMEM_LIMIT),
    )(
        *[in_memory(v) if i in loaded and i not in free else v for i, v in enumerate(operands)],
        *waits,
        *[in_memory(value) for value in held],
    )


def exchange(value, axes):
    return lax.all_to_all(value, axes, 0, 0, tiled=True)


def over_all(payload, kind, waits=(), held=()):
    first = exchange(payload, FIRST_STAGE)
    (merged,) = call(
        functools.partial(k_merge, kind),
        [(payload.shape, F32)],
        first,
        waits=waits,
        held=held,
        name="merge_" + kind,
    )
    return exchange(merged, SECOND_STAGE), merged


def passed_along(value, steps):
    count = 128
    leading, last = (max(0, -steps), min(count, count - steps))
    return lax.ppermute(value, SEQ, [(source, source + steps) for source in range(leading, last)])


def neighbours(rows, dilation):
    hops = dilation // 64
    return passed_along(rows, hops), passed_along(rows, -hops)


def chip_share(*pairs, waits=(), waits_first=(), held=()):
    operands = [value for pair in pairs for value in pair]
    width = sum(right.shape[1] for _, right in pairs) // 2
    shape = [((CH, width), BF16)]
    flops = 2 * ROWS * CH * width
    count = len(operands)
    (given,) = call(
        k_give,
        shape,
        *operands,
        loaded=tuple(range(count)),
        waits=waits_first,
        name="give",
        flops=flops,
    )
    arrived = swapped(given, "dp", 1)
    (share,) = call(
        functools.partial(k_keep, len(pairs)),
        shape,
        arrived,
        *operands,
        loaded=tuple(range(1, count + 1)),
        stored=(0,),
        waits=waits,
        held=held,
        name="keep",
        flops=flops,
    )
    return share


def swapped(value, axis, step):
    pairs = [(i, i ^ step) for i in range(SIZES[axis])]
    return lax.ppermute(value, axis, pairs)


def rows_over(share, axis):
    return lax.psum_scatter(share, axis, scatter_dimension=0, tiled=True)


def on_device(
    activations,
    segment_ids,
    interval_bounds,
    conv_weight,
    proj_weight,
    gains_in,
    biases_in,
    gains_mid,
    biases_mid,
    cotangent,
):
    windows, local_bins, channels = activations.shape
    position = lax.axis_index(SEQ) * local_bins + jnp.arange(local_bins, dtype=jnp.int32)[None, :]
    labels = jnp.arange(interval_bounds.shape[1] - 1, dtype=jnp.int32)
    matches = segment_ids[:, :, None] == labels[None, None, :]
    starts = jnp.sum(jnp.where(matches, interval_bounds[:, None, :-1], 0), axis=2)
    finishes = jnp.sum(jnp.where(matches, interval_bounds[:, None, 1:], 0), axis=2)
    masks = []
    for dilation in (FIRST_DILATION, SECOND_DILATION):
        masks.append(starts <= position - dilation)
        masks.append(position + dilation < finishes)
    masks = jnp.stack(masks, axis=2).astype(F32).reshape(ROWS, 4)

    wide, narrow = (GROUP, 1, 2 * CH), (GROUP, 1, CH)
    conv_flops = 2 * ROWS * CH * 3 * HALF
    stream_0 = activations.reshape(ROWS, CH)
    grad_2 = cotangent.reshape(ROWS, CH)

    def entry(layer, stream, parts, sides):
        return call(
            functools.partial(k_entry, layer),
            [((ROWS, CH), BF16), ((ROWS, CH), F32), ((ROWS, HALF), F32), ((2, CH), F32), (narrow, F32)],
            parts,
            stream,
            *sides,
            masks,
            conv_weight,
            gains_in,
            biases_in,
            loaded=(5, 6, 7) if layer else (1, 5, 6, 7),
            free=(6, 7) if layer else (),
            stored=(0, 1, 3),
            layers={5: layer},
            name="entry",
            flops=conv_flops,
        )

    (payload,) = call(k_first, [(wide, F32)], stream_0, loaded=(0,), name="first")
    merged, sent = call(
        k_merge_first,
        [(wide, F32), ((ROWS, CH), BF16)],
        exchange(payload, FIRST_STAGE),
        stream_0,
        loaded=(1,),
        free=(1,),
        name="merge_moments",
    )
    sides = neighbours(sent, FIRST_DILATION)
    parts = exchange(merged, SECOND_STAGE)
    taps_0, slope_0, conv_0, stat_0, payload = entry(0, stream_0, parts, sides)
    parts, _ = over_all(payload, "moments")
    hidden_0, stream_1, kept_1, slope_mid_0, normed_0, factor_0, payload = call(
        k_middle,
        [
            ((ROWS, HALF), BF16),
            ((ROWS, CH), BF16),
            ((ROWS, CH), BF16),
            ((ROWS, HALF), F32),
            ((ROWS, HALF), F32),
            ((1, HALF), F32),
            (wide, F32),
        ],
        parts,
        conv_0,
        gains_mid,
        biases_mid,
        proj_weight,
        stream_0,
        loaded=(2, 3, 4, 5),
        free=(2, 3, 4, 5),
        stored=(0, 2, 3, 4, 5),
        layers={4: 0},
        name="middle",
    )
    sides = neighbours(stream_1, SECOND_DILATION)
    parts, _ = over_all(payload, "moments", sides)
    taps_1, slope_1, conv_1, stat_1, payload = entry(1, stream_1, parts, sides)
    parts, _ = over_all(payload, "moments")
    hidden_1, stream_2, normed_1, factor_1, grad, pair, payload = call(
        k_turn,
        [
            ((ROWS, HALF), BF16),
            ((ROWS, CH), BF16),
            ((ROWS, HALF), F32),
            ((1, HALF), F32),
            ((ROWS, HALF), F32),
            ((ROWS, CH), BF16),
            (narrow, F32),
        ],
        parts,
        conv_1,
        gains_mid,
        biases_mid,
        proj_weight,
        kept_1,
        grad_2,
        loaded=(2, 3, 4, 5, 6),
        free=(2, 3, 4, 5, 6),
        stored=(0, 1),
        layers={4: 1},
        name="turn",
    )

    def back_middle(
        layer, parts, grad, normed, factor, sides, slope, stream, stat, *given, held=()
    ):
        rows = 2 - layer
        return call(
            functools.partial(k_back_middle, layer),
            [
                ((ROWS, 3 * HALF), BF16),
                ((ROWS, CH), F32),
                ((rows, HALF), F32),
                ((rows, HALF), F32),
                (wide if layer else (1, 1, 2 * CH), F32),
            ],
            parts,
            grad,
            normed,
            factor,
            *sides,
            masks,
            gains_mid,
            conv_weight,
            slope,
            stream,
            stat,
            *given,
            loaded=(7, 8, 9, 10, 11) if layer else (2, 3, 7, 8, 9, 10, 11, 12, 13),
            free=(7, 9, 10, 11) if layer else (2, 3, 7, 9, 10, 11, 12, 13),
            stored=(0, 2, 3),
            layers={8: layer},
            held=held,
            name="back_middle",
            flops=conv_flops,
        )

    sides = neighbours(pair, SECOND_DILATION)
    parts, _ = over_all(payload, "sums", sides)
    three_1, grad_in, gain_mid, bias_mid, payload = back_middle(
        1, parts, grad, normed_1, factor_1, sides, slope_1, kept_1, stat_1
    )
    parts, merged_1 = over_all(payload, "sums")
    gain_in, bias_in, grad_1, grad, pair, payload = call(
        k_back_entry,
        [
            ((1, CH), F32),
            ((1, CH), F32),
            ((ROWS, CH), BF16),
            ((ROWS, HALF), F32),
            ((ROWS, CH), BF16),
            (narrow, F32),
        ],
        parts,
        grad_in,
        kept_1,
        stat_1,
        gains_in,
        grad_2,
        proj_weight,
        slope_mid_0,
        normed_0,
        loaded=(2, 3, 4, 5, 6, 7, 8),
        free=(2, 3, 4, 5, 6, 7, 8),
        stored=(0, 1, 2),
        layers={6: 0},
        name="back_entry",
    )
    sides = neighbours(pair, FIRST_DILATION)
    parts, merged_0 = over_all(payload, "sums", sides)
    share_1 = chip_share(
        (taps_1, three_1), (grad_2, hidden_1), waits_first=(merged_1,), waits=(merged_0,)
    )
    rows_1 = rows_over(share_1, "y")
    three_0, grad_in, grad_gains_mid, grad_biases_mid, payload = back_middle(
        0,
        parts,
        grad,
        normed_0,
        factor_0,
        sides,
        slope_0,
        stream_0,
        stat_0,
        gain_mid,
        bias_mid,
    )
    share_0 = chip_share((taps_0, three_0), (grad_1, hidden_0))
    (sums,) = call(k_pass, [(payload.shape, F32)], payload, held=(share_0,), name="pass_sums")
    for axis, step in (("dp", 1), ("z", 1), ("z", 2), ("z", 4)):
        sums = sums + swapped(sums, axis, step)
    near = sums
    for axis, step in (("x", 1), ("x", 2), ("y", 1), ("y", 2)):
        sums = sums + swapped(sums, axis, step)
    (rows_1,) = call(
        k_pass,
        [(rows_1.shape, BF16)],
        rows_1,
        loaded=(0,),
        stored=(0,),
        held=(share_0,),
        name="pass",
    )
    rows_1 = rows_over(rows_1, "x")
    share_0 = exchange(share_0.reshape(GROUP, CH // GROUP, CH), SECOND_STAGE)
    grad_gains_in, grad_biases_in, grad_0 = call(
        k_last,
        [((2, CH), F32), ((2, CH), F32), ((ROWS, CH), BF16)],
        sums,
        grad_in,
        stream_0,
        stat_0,
        gains_in,
        grad_1,
        gain_in,
        bias_in,
        loaded=(2, 3, 4, 5, 6, 7),
        free=(2, 3, 4, 5, 6, 7),
        stored=(0, 1, 2),
        name="last",
    )
    (rows,) = call(
        k_gather,
        [((GROUP, 8, 2 * CH), BF16)],
        share_0,
        rows_1,
        loaded=(1,),
        waits=(near,),
        name="gather_rows",
    )
    grad_conv, grad_proj = call(
        k_rows,
        [((2, 8, 3 * HALF), F32), ((2, 8, HALF), F32)],
        exchange(rows, FIRST_STAGE),
        stored=(0, 1),
        name="rows",
    )
    return (
        stream_2.reshape(activations.shape),
        grad_0.reshape(activations.shape),
        grad_conv,
        grad_proj,
        grad_gains_in,
        grad_biases_in,
        grad_gains_mid,
        grad_biases_mid,
    )


def solution(mesh):
    sizes = tuple(SIZES.values())
    split = Mesh(mesh.devices.reshape(sizes), tuple(SIZES))
    bins = P("dp", SEQ, None)
    rows = P(None, SEQ, None)
    in_specs = (bins, P("dp", SEQ), P("dp", None), P(), P(), P(), P(), P(), P(), bins)
    out_specs = (bins, bins, rows, rows, P(), P(), P(), P())
    return jax.shard_map(
        on_device, mesh=split, in_specs=in_specs, out_specs=out_specs, check_vma=False
    )
```

```python
import functools

import jax
import jax.numpy as jnp
from jax import lax
from jax.experimental import pallas as pl
from jax.experimental.pallas import tpu as pltpu
from jax.sharding import Mesh, PartitionSpec as P

FIRST_DILATION = 64
SECOND_DILATION = 512
EPSILON = 1e-05
SIZES = {"dp": 2, "y": 4, "x": 4, "z": 8}
SEQ = ("y", "x", "z")
FIRST_STAGE = ("dp", "z")
SECOND_STAGE = ("y", "x")
GROUP = 16
F32 = jnp.float32
BF16 = jnp.bfloat16
ROWS, CH, HALF = 128, 1024, 512
VMEM_LIMIT = 32 << 20
PIECES = 4
TOTAL = 32768.0
TANH_SCALE = 0.7978845608028654
CUBE = 0.044715


def gelu(v):
    return 0.5 * v * (1.0 + jnp.tanh(TANH_SCALE * (v + CUBE * (v * v * v))))


def gelu_slope(v):
    square = v * v
    t = jnp.tanh(TANH_SCALE * (v + CUBE * (square * v)))
    half = 0.5 * (1.0 + t)
    slope = half + 0.5 * v * (1.0 - t * t) * (TANH_SCALE * (1.0 + 3.0 * CUBE * square))
    return v * half, slope


def spread_out(out, first, second):
    row = jnp.concatenate([first, second], axis=1)
    for i in range(out.shape[0]):
        out[i] = row


def local_moments(values):
    mean = jnp.sum(values, axis=0, keepdims=True) * (1.0 / ROWS)
    centred = values - mean
    return mean, jnp.sum(centred * centred, axis=0, keepdims=True) * (1.0 / ROWS)


def merged_moments(parts):
    width = parts.shape[2] // 2
    means = [parts[i, :, :width] for i in range(GROUP)]
    mean = sum(means[1:], means[0]) * (1.0 / GROUP)
    square = jnp.zeros_like(mean)
    for i in range(GROUP):
        offset = means[i] - mean
        square = square + (parts[i, :, width:] + offset * offset)
    return mean, square * (1.0 / GROUP)


def merged_sums(parts):
    width = parts.shape[2] // 2
    total = parts[0]
    for i in range(1, GROUP):
        total = total + parts[i]
    return total[:, :width], total[:, width:]


def product(left, right):
    return jnp.dot(left, right, preferred_element_type=F32)


def product_nt(left, right):
    return lax.dot_general(left, right, (((1,), (1,)), ((), ())), preferred_element_type=F32)


def product_tn(left, right):
    return lax.dot_general(left, right, (((0,), (0,)), ((), ())), preferred_element_type=F32)


def k_first(x, out):
    spread_out(out, *local_moments(x[...].astype(F32)))


def k_merge(kind, parts, out):
    merge = merged_moments if kind == "moments" else merged_sums
    spread_out(out, *merge(parts))


def k_entry(layer, parts, x, lower, upper, masks, weight, gains, biases, taps, slope, conv, stat, out):
    mean, spread = merged_moments(parts)
    factor = lax.rsqrt(spread + EPSILON)
    gain, bias = gains[layer : layer + 1], biases[layer : layer + 1]
    active, slope_in = gelu_slope((x[...].astype(F32) - mean) * factor * gain + bias)
    slope[...] = slope_in
    centre = active.astype(BF16)
    taps[...] = centre
    stat[...] = jnp.concatenate([mean, factor], axis=0)

    def side(rows, column):
        values = gelu((rows[...].astype(F32) - mean) * factor * gain + bias)
        mask = masks[:, 2 * layer + column : 2 * layer + column + 1]
        return jnp.where(mask > 0, values, 0.0).astype(BF16)

    result = product(centre, weight[:, HALF : 2 * HALF])
    result = result + product(side(lower, 0), weight[:, :HALF])
    result = result + product(side(upper, 1), weight[:, 2 * HALF :])
    conv[...] = result
    spread_out(out, *local_moments(result))


def middle(layer, parts, conv, gains, biases, project, x):
    mean, spread = merged_moments(parts)
    factor = lax.rsqrt(spread + EPSILON)
    normed = (conv[...] - mean) * factor
    active, slope = gelu_slope(normed * gains[layer : layer + 1] + biases[layer : layer + 1])
    hidden = active.astype(BF16)
    following = (x[...].astype(F32) + product_nt(hidden, project[...])).astype(BF16)
    return factor, normed, slope, hidden, following


def k_middle(
    parts, conv, gains, biases, project, x, hidden, following, kept, slope, normed, factor, out
):
    factor[...], normed[...], slope[...], hidden[...], rows = middle(
        0, parts, conv, gains, biases, project, x
    )
    following[...] = rows
    kept[...] = rows
    spread_out(out, *local_moments(rows.astype(F32)))


def begin_backward(upstream, project, slope, normed, grad, pair, out):
    values = product(upstream, project[...]) * slope
    grad[...] = values
    pair[:, :HALF] = values.astype(BF16)
    pair[:, HALF:] = normed.astype(BF16)
    spread_out(
        out,
        jnp.sum(values, axis=0, keepdims=True),
        jnp.sum(values * normed, axis=0, keepdims=True),
    )


def k_turn(parts, conv, gains, biases, project, x, upstream, hidden, following, normed, factor, grad, pair, out):
    factor[...], rows, slope, hidden[...], following[...] = middle(
        1, parts, conv, gains, biases, project, x
    )
    normed[...] = rows
    begin_backward(upstream[...], project, slope, rows, grad, pair, out)


def k_back_middle(
    layer, parts, grad, normed, factor, lower, upper, masks, gains, weight, slope, x, stat, *rest
):
    if layer == 0:
        given_gain, given_bias, three, grad_in, gain_out, bias_out, out = rest
    else:
        three, grad_in, gain_out, bias_out, out = rest
    total, cross = merged_sums(parts)
    gain_out[0:1] = cross
    bias_out[0:1] = total
    if layer == 0:
        gain_out[1:2] = given_gain[...]
        bias_out[1:2] = given_bias[...]
    total, cross = total * (1.0 / TOTAL), cross * (1.0 / TOTAL)
    scale = gains[layer : layer + 1] * factor[...]

    def conv_grad(grads, rows):
        return scale * (grads - total - rows * cross)

    def side(pair, column):
        values = conv_grad(pair[:, :HALF].astype(F32), pair[:, HALF:].astype(F32))
        mask = masks[:, 2 * layer + column : 2 * layer + column + 1]
        return jnp.where(mask > 0, values, 0.0).astype(BF16)

    three[:, :HALF] = side(upper, 1)
    three[:, HALF : 2 * HALF] = conv_grad(grad[...], normed[...]).astype(BF16)
    three[:, 2 * HALF :] = side(lower, 0)
    values = product_nt(three[...], weight[...]) * slope[...]
    grad_in[...] = values
    normed_in = (x[...].astype(F32) - stat[0:1]) * stat[1:2]
    spread_out(
        out,
        jnp.sum(values, axis=0, keepdims=True),
        jnp.sum(values * normed_in, axis=0, keepdims=True),
    )


def back_entry(layer, parts, grad_in, x, stat, gains, upstream):
    if layer == 0:
        total, cross = parts[0, :, :CH], parts[0, :, CH:]
    else:
        total, cross = merged_sums(parts)
    factor = stat[1:2]
    normed = (x[...].astype(F32) - stat[0:1]) * factor
    branch = (gains[layer : layer + 1] * factor) * (
        grad_in[...] - total * (1.0 / TOTAL) - normed * (cross * (1.0 / TOTAL))
    )
    return total, cross, (upstream[...].astype(F32) + branch).astype(BF16)


def k_back_entry(
    parts, grad_in, x, stat, gains, upstream, project, slope, normed, *rest
):
    gain_out, bias_out, stream, grad, pair, out = rest
    bias_out[...], gain_out[...], rows = back_entry(1, parts, grad_in, x, stat, gains, upstream)
    stream[...] = rows
    begin_backward(rows, project, slope[...], normed[...], grad, pair, out)


def k_last(parts, grad_in, x, stat, gains, upstream, given_gain, given_bias, gain_out, bias_out, stream):
    total, cross, stream[...] = back_entry(0, parts, grad_in, x, stat, gains, upstream)
    gain_out[0:1] = cross
    gain_out[1:2] = given_gain[...]
    bias_out[0:1] = total
    bias_out[1:2] = given_bias[...]


def half_of(ref, other):
    half = ref.shape[1] // 2
    place = lax.axis_index("dp")
    place = 1 - place if other else place
    return ref[:, pl.ds(pl.multiple_of(place * half, 128), half)]


def k_give(*refs):
    out, first = refs[-1], 0
    for left, right in zip(refs[0:-1:2], refs[1:-1:2]):
        width = right.shape[1] // 2
        out[:, first : first + width] = product_tn(left[...], half_of(right, True)).astype(BF16)
        first += width


def k_keep(pairs, arrived, *refs):
    out = refs[-1]
    count = CH // PIECES
    for piece in range(PIECES):
        rows, first = slice(piece * count, (piece + 1) * count), 0
        for i in range(pairs):
            left, right = refs[2 * i], refs[2 * i + 1]
            width = right.shape[1] // 2
            other = arrived[rows, first : first + width].astype(F32)
            mine = product_tn(left[:, rows], half_of(right, False))
            out[rows, first : first + width] = (mine + other).astype(BF16)
            first += width
        out.send_rows(rows)


def k_gather(parts, other, out):
    for z in range(8):
        rows = slice(8 * z, 8 * z + 8)
        total = parts[0, rows].astype(F32)
        for i in range(1, GROUP):
            total = total + parts[i, rows].astype(F32)
        whole_row = jnp.concatenate([total.astype(BF16), other[rows, :]], axis=1)
        out[z] = whole_row
        out[8 + z] = whole_row


def k_rows(parts, kernel_out, project_out):
    cut, width = 3 * HALF // 2, HALF // 2
    for d in range(2):
        total = parts[8 * d].astype(F32)
        for z in range(1, 8):
            total = total + parts[8 * d + z].astype(F32)
        for layer in range(2):
            first = layer * CH
            kernel_out[layer, :, d * cut : (d + 1) * cut] = total[:, first : first + cut]
            project_out[layer, :, d * width : (d + 1) * width] = total[:, first + cut : first + CH]


def k_pass(value, out):
    out[...] = value[...]


def whole(value):
    shape = value.shape
    return pl.BlockSpec(shape, lambda i: (0,) * len(shape))


def in_memory(value):
    return pltpu.with_memory_space_constraint(value, pltpu.HBM)


class Loaded:
    def __init__(self, copy, ref):
        self.copy, self.ref, self.shape = copy, ref, ref.shape
        copy.start()

    def finish(self):
        if self.copy is not None:
            self.copy.wait()
            self.copy = None

    def __getitem__(self, place):
        self.finish()
        return self.ref[place]


class Stored:
    def __init__(self, ref, target, sems):
        self.ref, self.target, self.sems, self.shape = ref, target, sems, ref.shape
        self.copies = []

    def send(self, source, target):
        self.copies.append(pltpu.make_async_copy(source, target, self.sems[len(self.copies)]))
        self.copies[-1].start()

    def send_rows(self, rows):
        self.send(self.ref.at[rows], self.target.at[rows])

    def start(self):
        if not self.copies:
            self.send(self.ref, self.target)

    def __getitem__(self, place):
        return self.ref[place]

    def __setitem__(self, place, value):
        self.ref[place] = value
        if place is Ellipsis:
            self.start()


def staged(kernel, counts, loaded, stored):
    n_in, n_waits, n_out = counts

    def body(*refs):
        ins, outs = list(refs[:n_in]), list(refs[n_in + n_waits : n_in + n_waits + n_out])
        scratch = list(refs[n_in + n_waits + n_out :])
        sems, late, results = scratch.pop(), [], []
        for place, (i, layer) in enumerate(loaded):
            source = ins[i] if layer is None else ins[i].at[layer]
            buffer = scratch.pop(0)
            ins[i] = Loaded(pltpu.make_async_copy(source, buffer, sems.at[place]), buffer)
            late.append(ins[i])
        for place, i in enumerate(stored):
            first = len(loaded) + PIECES * place
            own = [sems.at[first + piece] for piece in range(PIECES)]
            outs[i] = Stored(scratch.pop(0), outs[i], own)
            results.append(outs[i])
        kernel(*ins, *outs)
        for value in late:
            value.finish()
        for value in results:
            value.start()
        for value in results:
            for copy in value.copies:
                copy.wait()

    return body


def call(kernel, outs, *operands, name, loaded=(), free=(), stored=(), layers=None, waits=(), held=(), flops=1 << 22):
    layers = layers or {}
    in_hbm = pl.BlockSpec(memory_space=pltpu.HBM)
    specs = [
        pl.BlockSpec(memory_space=pl.ANY) if i in free else in_hbm if i in loaded else whole(value)
        for i, value in enumerate(operands)
    ]
    specs += [pl.BlockSpec(memory_space=pl.ANY)] * len(waits) + [in_hbm] * len(held)
    shapes = [jax.ShapeDtypeStruct(shape, dtype) for shape, dtype in outs]
    moved = sum(v.size * v.dtype.itemsize for v in list(operands) + shapes)
    scratch = []
    for i in loaded:
        shape = operands[i].shape
        scratch.append(pltpu.VMEM(shape[1:] if i in layers else shape, operands[i].dtype))
    scratch += [pltpu.VMEM(*outs[i]) for i in stored]
    scratch.append(pltpu.SemaphoreType.DMA((max(1, len(loaded) + PIECES * len(stored)),)))
    body = staged(
        kernel,
        (len(operands), len(waits) + len(held), len(outs)),
        [(i, layers.get(i)) for i in loaded],
        stored,
    )
    return pl.pallas_call(
        body,
        grid=(1,),
        in_specs=specs,
        out_specs=[in_hbm if i in stored else whole(shape) for i, shape in enumerate(shapes)],
        out_shape=[
            pltpu.HBM(shape.shape, shape.dtype) if i in stored else shape
            for i, shape in enumerate(shapes)
        ],
        scratch_shapes=scratch,
        name=name,
        cost_estimate=pl.CostEstimate(flops=flops, bytes_accessed=moved, transcendentals=0),
        compiler_params=pltpu.CompilerParams(vmem_limit_bytes=VMEM_LIMIT),
    )(
        *[in_memory(v) if i in loaded and i not in free else v for i, v in enumerate(operands)],
        *waits,
        *[in_memory(value) for value in held],
    )


def exchange(value, axes):
    return lax.all_to_all(value, axes, 0, 0, tiled=True)


def over_all(payload, kind, waits=(), held=()):
    first = exchange(payload, FIRST_STAGE)
    (merged,) = call(
        functools.partial(k_merge, kind),
        [(payload.shape, F32)],
        first,
        waits=waits,
        held=held,
        name="merge_" + kind,
    )
    return exchange(merged, SECOND_STAGE), merged


def passed_along(value, steps):
    count = 128
    leading, last = (max(0, -steps), min(count, count - steps))
    return lax.ppermute(value, SEQ, [(source, source + steps) for source in range(leading, last)])


def neighbours(rows, dilation):
    hops = dilation // 64
    return passed_along(rows, hops), passed_along(rows, -hops)


def chip_share(*pairs, waits=(), waits_first=(), held=()):
    operands = [value for pair in pairs for value in pair]
    width = sum(right.shape[1] for _, right in pairs) // 2
    shape = [((CH, width), BF16)]
    flops = 2 * ROWS * CH * width
    count = len(operands)
    (given,) = call(
        k_give,
        shape,
        *operands,
        loaded=tuple(range(count)),
        waits=waits_first,
        name="give",
        flops=flops,
    )
    arrived = swapped(given, "dp", 1)
    (share,) = call(
        functools.partial(k_keep, len(pairs)),
        shape,
        arrived,
        *operands,
        loaded=tuple(range(1, count + 1)),
        stored=(0,),
        waits=waits,
        held=held,
        name="keep",
        flops=flops,
    )
    return share


def swapped(value, axis, step):
    pairs = [(i, i ^ step) for i in range(SIZES[axis])]
    return lax.ppermute(value, axis, pairs)


def rows_over(share, axis):
    return lax.psum_scatter(share, axis, scatter_dimension=0, tiled=True)


def on_device(
    activations,
    segment_ids,
    interval_bounds,
    conv_weight,
    proj_weight,
    gains_in,
    biases_in,
    gains_mid,
    biases_mid,
    cotangent,
):
    windows, local_bins, channels = activations.shape
    position = lax.axis_index(SEQ) * local_bins + jnp.arange(local_bins, dtype=jnp.int32)[None, :]
    labels = jnp.arange(interval_bounds.shape[1] - 1, dtype=jnp.int32)
    matches = segment_ids[:, :, None] == labels[None, None, :]
    starts = jnp.sum(jnp.where(matches, interval_bounds[:, None, :-1], 0), axis=2)
    finishes = jnp.sum(jnp.where(matches, interval_bounds[:, None, 1:], 0), axis=2)
    masks = []
    for dilation in (FIRST_DILATION, SECOND_DILATION):
        masks.append(starts <= position - dilation)
        masks.append(position + dilation < finishes)
    masks = jnp.stack(masks, axis=2).astype(F32).reshape(ROWS, 4)

    wide, narrow = (GROUP, 1, 2 * CH), (GROUP, 1, CH)
    conv_flops = 2 * ROWS * CH * 3 * HALF
    stream_0 = activations.reshape(ROWS, CH)
    grad_2 = cotangent.reshape(ROWS, CH)

    def entry(layer, stream, parts, sides):
        return call(
            functools.partial(k_entry, layer),
            [((ROWS, CH), BF16), ((ROWS, CH), F32), ((ROWS, HALF), F32), ((2, CH), F32), (narrow, F32)],
            parts,
            stream,
            *sides,
            masks,
            conv_weight,
            gains_in,
            biases_in,
            loaded=(5, 6, 7) if layer else (1, 5, 6, 7),
            free=(6, 7) if layer else (),
            stored=(0, 1, 3),
            layers={5: layer},
            name="entry",
            flops=conv_flops,
        )

    (payload,) = call(k_first, [(wide, F32)], stream_0, loaded=(0,), name="first")
    sides = neighbours(stream_0, FIRST_DILATION)
    parts, _ = over_all(payload, "moments", sides)
    taps_0, slope_0, conv_0, stat_0, payload = entry(0, stream_0, parts, sides)
    parts, _ = over_all(payload, "moments")
    hidden_0, stream_1, kept_1, slope_mid_0, normed_0, factor_0, payload = call(
        k_middle,
        [
            ((ROWS, HALF), BF16),
            ((ROWS, CH), BF16),
            ((ROWS, CH), BF16),
            ((ROWS, HALF), F32),
            ((ROWS, HALF), F32),
            ((1, HALF), F32),
            (wide, F32),
        ],
        parts,
        conv_0,
        gains_mid,
        biases_mid,
        proj_weight,
        stream_0,
        loaded=(2, 3, 4, 5),
        free=(2, 3, 4, 5),
        stored=(0, 2, 3, 4, 5),
        layers={4: 0},
        name="middle",
    )
    sides = neighbours(stream_1, SECOND_DILATION)
    parts, _ = over_all(payload, "moments", sides)
    taps_1, slope_1, conv_1, stat_1, payload = entry(1, stream_1, parts, sides)
    parts, _ = over_all(payload, "moments")
    hidden_1, stream_2, normed_1, factor_1, grad, pair, payload = call(
        k_turn,
        [
            ((ROWS, HALF), BF16),
            ((ROWS, CH), BF16),
            ((ROWS, HALF), F32),
            ((1, HALF), F32),
            ((ROWS, HALF), F32),
            ((ROWS, CH), BF16),
            (narrow, F32),
        ],
        parts,
        conv_1,
        gains_mid,
        biases_mid,
        proj_weight,
        kept_1,
        grad_2,
        loaded=(2, 3, 4, 5, 6),
        free=(2, 3, 4, 5, 6),
        stored=(0, 1),
        layers={4: 1},
        name="turn",
    )

    def back_middle(
        layer, parts, grad, normed, factor, sides, slope, stream, stat, *given, held=()
    ):
        rows = 2 - layer
        return call(
            functools.partial(k_back_middle, layer),
            [
                ((ROWS, 3 * HALF), BF16),
                ((ROWS, CH), F32),
                ((rows, HALF), F32),
                ((rows, HALF), F32),
                (wide if layer else (1, 1, 2 * CH), F32),
            ],
            parts,
            grad,
            normed,
            factor,
            *sides,
            masks,
            gains_mid,
            conv_weight,
            slope,
            stream,
            stat,
            *given,
            loaded=(7, 8, 9, 10, 11) if layer else (2, 3, 7, 8, 9, 10, 11, 12, 13),
            free=(7, 9, 10, 11) if layer else (2, 3, 7, 9, 10, 11, 12, 13),
            stored=(0, 2, 3),
            layers={8: layer},
            held=held,
            name="back_middle",
            flops=conv_flops,
        )

    sides = neighbours(pair, SECOND_DILATION)
    parts, _ = over_all(payload, "sums", sides)
    three_1, grad_in, gain_mid, bias_mid, payload = back_middle(
        1, parts, grad, normed_1, factor_1, sides, slope_1, kept_1, stat_1
    )
    parts, merged_1 = over_all(payload, "sums")
    gain_in, bias_in, grad_1, grad, pair, payload = call(
        k_back_entry,
        [
            ((1, CH), F32),
            ((1, CH), F32),
            ((ROWS, CH), BF16),
            ((ROWS, HALF), F32),
            ((ROWS, CH), BF16),
            (narrow, F32),
        ],
        parts,
        grad_in,
        kept_1,
        stat_1,
        gains_in,
        grad_2,
        proj_weight,
        slope_mid_0,
        normed_0,
        loaded=(2, 3, 4, 5, 6, 7, 8),
        free=(2, 3, 4, 5, 6, 7, 8),
        stored=(0, 1, 2),
        layers={6: 0},
        name="back_entry",
    )
    sides = neighbours(pair, FIRST_DILATION)
    parts, merged_0 = over_all(payload, "sums", sides)
    share_1 = chip_share(
        (taps_1, three_1), (grad_2, hidden_1), waits_first=(merged_1,), waits=(merged_0,)
    )
    rows_1 = rows_over(share_1, "y")
    three_0, grad_in, grad_gains_mid, grad_biases_mid, payload = back_middle(
        0,
        parts,
        grad,
        normed_0,
        factor_0,
        sides,
        slope_0,
        stream_0,
        stat_0,
        gain_mid,
        bias_mid,
    )
    share_0 = chip_share((taps_0, three_0), (grad_1, hidden_0))
    (sums,) = call(k_pass, [(payload.shape, F32)], payload, held=(share_0,), name="pass_sums")
    for axis, step in (("dp", 1), ("z", 1), ("z", 2), ("z", 4)):
        sums = sums + swapped(sums, axis, step)
    near = sums
    for axis, step in (("x", 1), ("x", 2), ("y", 1), ("y", 2)):
        sums = sums + swapped(sums, axis, step)
    (rows_1,) = call(
        k_pass,
        [(rows_1.shape, BF16)],
        rows_1,
        loaded=(0,),
        stored=(0,),
        held=(share_0,),
        name="pass",
    )
    rows_1 = rows_over(rows_1, "x")
    share_0 = exchange(share_0.reshape(GROUP, CH // GROUP, CH), SECOND_STAGE)
    grad_gains_in, grad_biases_in, grad_0 = call(
        k_last,
        [((2, CH), F32), ((2, CH), F32), ((ROWS, CH), BF16)],
        sums,
        grad_in,
        stream_0,
        stat_0,
        gains_in,
        grad_1,
        gain_in,
        bias_in,
        loaded=(2, 3, 4, 5, 6, 7),
        free=(2, 3, 4, 5, 6, 7),
        stored=(0, 1, 2),
        name="last",
    )
    (rows,) = call(
        k_gather,
        [((GROUP, 8, 2 * CH), BF16)],
        share_0,
        rows_1,
        loaded=(1,),
        waits=(near,),
        name="gather_rows",
    )
    grad_conv, grad_proj = call(
        k_rows,
        [((2, 8, 3 * HALF), F32), ((2, 8, HALF), F32)],
        exchange(rows, FIRST_STAGE),
        stored=(0, 1),
        name="rows",
    )
    return (
        stream_2.reshape(activations.shape),
        grad_0.reshape(activations.shape),
        grad_conv,
        grad_proj,
        grad_gains_in,
        grad_biases_in,
        grad_gains_mid,
        grad_biases_mid,
    )


def solution(mesh):
    sizes = tuple(SIZES.values())
    split = Mesh(mesh.devices.reshape(sizes), tuple(SIZES))
    bins = P("dp", SEQ, None)
    rows = P(None, SEQ, None)
    in_specs = (bins, P("dp", SEQ), P("dp", None), P(), P(), P(), P(), P(), P(), bins)
    out_specs = (bins, bins, rows, rows, P(), P(), P(), P())
    return jax.shard_map(
        on_device, mesh=split, in_specs=in_specs, out_specs=out_specs, check_vma=False
    )
```
